32 devices in a mesh: dp: 8 (over y, x, core), tensor: 4 (over z).
Axes of the slice: x: 2, y: 2, z: 4, core: 2. Of those that a mesh axis runs over, the one named last changes fastest.
Arguments:
- inputs: bfloat16 [8192, 1024], P('dp', 'tensor'), may hold values from -6 to 6
- lengths: int32 [8], P('dp'), may hold values from 512 to 1024, as said below
- random_blocks: int32 [8, 16, 16, 3], P('dp', 'tensor'), may hold values from 1 to 14
- attn_norm_gain: bfloat16 [1024], P('tensor'), may hold values from 0.5 to 1.5
- attn_norm_bias: bfloat16 [1024], P('tensor'), may hold values from -1.75 to 1.75
- query_weight: bfloat16 [1024, 1024], P(None, 'tensor'), may hold values from -0.1875 to 0.1875
- query_bias: bfloat16 [1024], P('tensor'), may hold values from -1.75 to 1.75
- key_weight: bfloat16 [1024, 1024], P(None, 'tensor'), may hold values from -0.1875 to 0.1875
- value_weight: bfloat16 [1024, 1024], P(None, 'tensor'), may hold values from -0.1875 to 0.1875
- value_bias: bfloat16 [1024], P('tensor'), may hold values from -1.75 to 1.75
- out_weight: bfloat16 [1024, 1024], P('tensor'), may hold values from -2 to 2
- out_bias: bfloat16 [1024], P('tensor'), may hold values from -1.75 to 1.75
- ffn_norm_gain: bfloat16 [1024], P('tensor'), may hold values from 0.2 to 2.2
- ffn_norm_bias: bfloat16 [1024], P('tensor'), may hold values from -1.75 to 1.75
- up_weight: bfloat16 [1024, 4096], P(None, 'tensor'), may hold values from -1 to 1
- up_bias: bfloat16 [4096], P('tensor'), may hold values from -1.75 to 1.75
- down_weight: bfloat16 [4096, 1024], P('tensor'), may hold values from -0.09375 to 0.09375
- down_bias: bfloat16 [1024], P('tensor'), may hold values from -1.75 to 1.75
- grad_out: bfloat16 [8192, 1024], P('dp', 'tensor'), may hold values from -6 to 6
Outputs:
- outputs: bfloat16 [8192, 1024], P('dp', 'tensor')
- grad_inputs: bfloat16 [8192, 1024], P('dp', 'tensor')
- grad_attn_norm_gain: float32 [1024], P('tensor')
- grad_attn_norm_bias: float32 [1024], P('tensor')
- grad_query_weight: float32 [1024, 1024], P(None, 'tensor')
- grad_query_bias: float32 [1024], P('tensor')
- grad_key_weight: float32 [1024, 1024], P(None, 'tensor')
- grad_value_weight: float32 [1024, 1024], P(None, 'tensor')
- grad_value_bias: float32 [1024], P('tensor')
- grad_out_weight: float32 [1024, 1024], P('tensor')
- grad_out_bias: float32 [1024], P('tensor')
- grad_ffn_norm_gain: float32 [1024], P('tensor')
- grad_ffn_norm_bias: float32 [1024], P('tensor')
- grad_up_weight: float32 [1024, 4096], P(None, 'tensor')
- grad_up_bias: float32 [4096], P('tensor')
- grad_down_weight: float32 [4096, 1024], P('tensor')
- grad_down_bias: float32 [1024], P('tensor')
The draws below stay inside these ranges and needn't reach their ends.
Inputs may be any that keep to these rules, and one draw needn't show every extreme that they name: `lengths`: valid tokens of each sequence; some sequence has exactly 1024.
All inputs are finite; a program needn't handle non-finite values.
Results may differ from the reference program's by a relative error of at most 0.018.
Values may be sent and summed in bfloat16 or wider, within the bound.
No kernel may reach another device: no remote copies, remote signals or barrier semaphores. Data moves between devices by JAX's collectives and lax.ppermute only.
A program may use at most 128 MiB of HBM per device.

```python
import jax
import jax.numpy as jnp
from jax import lax

D = 1024
H = 16
HD = 64
FF = 4096
BLOCK = 64
RAND = 3
LEN = 1024
SEQS = 8
TOKENS = 8192
NB = 16
QB = 512


def draw_lengths(key, part):
    key = jax.random.fold_in(key, 11)
    first_key, second_key = jax.random.split(key)
    drawn = jax.random.randint(first_key, (SEQS,), LEN // 2, LEN + 1)
    longest = jax.random.randint(second_key, (), 0, SEQS)
    return jnp.where(jnp.arange(SEQS) == longest, LEN, drawn).astype(jnp.int32)


def draw_ffn_norm_gain(key, part):
    key = jax.random.fold_in(key, 23)
    place = jnp.arange(D, dtype=jnp.float32) / (D - 1)
    rough = 1.0 + 0.1 * jnp.clip(jax.random.normal(key, (D,), jnp.float32), -2.0, 2.0)
    return ((0.5 + place) * rough).astype(jnp.bfloat16)


def draw_up_weight(key, part):
    key = jax.random.fold_in(key, 37)
    main_key, common_key = jax.random.split(key)
    common = jnp.clip(jax.random.normal(common_key, (1, FF), jnp.float32), -3.0, 3.0) / jnp.sqrt(D * 1.0)
    spread = jnp.clip(jax.random.normal(main_key, (D, FF), jnp.float32), -4.0, 4.0) / jnp.sqrt(D * 1.0)
    return (spread + common).astype(jnp.bfloat16)


def with_ends(values, own_key, least, largest):
    index_at = [jax.random.randint(jax.random.fold_in(own_key, axis), (), 0, length) for axis, length in enumerate(values.shape)]
    widest = values.shape.index(max(values.shape))
    neighbour = index_at[:widest] + [(index_at[widest] + 1) % values.shape[widest]] + index_at[widest + 1:]
    return values.at[tuple(index_at)].set(least).at[tuple(neighbour)].set(largest)


def levels(stream_key, dims, cuts, least, high):
    def one(dim, parts):
        steps = jax.random.uniform(jax.random.fold_in(jax.random.fold_in(stream_key, 6), dim), (parts,), jnp.float32, least / len(cuts), high / len(cuts))
        return jnp.repeat(jnp.exp(steps), dims[dim] // parts).reshape((-1,) + (1,) * (len(dims) - dim - 1))

    loudness = one(*cuts[0])
    for cut in cuts[1:]:
        loudness = loudness * one(*cut)
    return loudness


def scatter_about(key, dims, deviation, most, shards=(), kind=jnp.bfloat16):
    array = jax.random.normal(key, dims, jnp.float32) * deviation
    if len(shards) > 0:
        array = levels(key, dims, shards, -0.22, 0.18) * array
    return jnp.clip(array, min=-most, max=most).astype(kind)


def setup_inputs(seed: int = 0) -> dict:
    streams_of = jax.random.split(jax.random.key(seed), 20)
    return {
        "inputs": scatter_about(streams_of[0], (TOKENS, D), 1.0, 6.0, ((0, 8), (1, 4))),
        "lengths": draw_lengths(jax.random.fold_in(streams_of[19], 71), 0),
        "random_blocks": with_ends(jax.random.randint(streams_of[2], (SEQS, H, NB, RAND), 1, NB - 1), jax.random.fold_in(streams_of[2], 1), 1, (NB - 1) - 1).astype(jnp.int32),
        "attn_norm_gain": jnp.clip(1.0 + 0.1 * jax.random.normal(streams_of[3], (D,), jnp.float32), 0.5, 1.5).astype(jnp.bfloat16),
        "attn_norm_bias": scatter_about(streams_of[4], (D,), 0.3, 1.75, ((0, 4),)),
        "query_weight": scatter_about(streams_of[5], (D, D), D ** -0.5, 0.1875, ((1, 4),)),
        "query_bias": scatter_about(streams_of[6], (D,), 0.3, 1.75, ((0, 4),)),
        "key_weight": scatter_about(streams_of[7], (D, D), D ** -0.5, 0.1875, ((1, 4),)),
        "value_weight": scatter_about(streams_of[8], (D, D), D ** -0.5, 0.1875, ((1, 4),)),
        "value_bias": scatter_about(streams_of[9], (D,), 0.3, 1.75, ((0, 4),)),
        "out_weight": scatter_about(streams_of[10], (D, D), (max(D // 128, 1)) ** -0.5, 2.0, ((0, 4),)),
        "out_bias": scatter_about(streams_of[11], (D,), 0.3, 1.75, ((0, 4),)),
        "ffn_norm_gain": draw_ffn_norm_gain(jax.random.fold_in(streams_of[19], 71), 0),
        "ffn_norm_bias": scatter_about(streams_of[13], (D,), 0.3, 1.75, ((0, 4),)),
        "up_weight": draw_up_weight(jax.random.fold_in(streams_of[19], 71), 0),
        "up_bias": scatter_about(streams_of[15], (FF,), 0.3, 1.75, ((0, 4),)),
        "down_weight": scatter_about(streams_of[16], (FF, D), FF ** -0.5, 0.09375, ((0, 4),)),
        "down_bias": scatter_about(streams_of[17], (D,), 0.3, 1.75, ((0, 4),)),
        "grad_out": scatter_about(streams_of[18], (TOKENS, D), 1.0, 6.0, ((0, 8), (1, 4))),
    }


precise = lax.Precision.HIGHEST
eps_norm = 1e-05

@jax.custom_vjp
def low(v):
    return lax.optimization_barrier(v.astype(jnp.bfloat16)).astype(jnp.float32)

@jax.custom_vjp
def low_back(v):
    return v

def low_keep(v):
    return (low(v), None)

def low_pass(kept, grad):
    return (grad,)

def back_keep(v):
    return (v, None)

def back_low(kept, grad):
    return (low(grad),)
low.defvjp(low_keep, low_pass)
low_back.defvjp(back_keep, back_low)

def matmul(left, right):
    return jnp.dot(left, right, precision=precise)

def layer_norm(values, norm_gain, norm_shift):
    average = lax.optimization_barrier(jnp.mean(values, axis=-1, keepdims=True))
    centered = values - average
    spread = lax.optimization_barrier(jnp.mean(centered * centered, axis=-1, keepdims=True))
    return centered * lax.rsqrt(spread + eps_norm) * norm_gain + norm_shift

def block_allowed(random_rows):
    row_ids = jnp.arange(NB, dtype=jnp.int32)[:, None]
    col_ids = jnp.arange(NB, dtype=jnp.int32)[None, :]
    fixed_part = (row_ids == 0) | (row_ids == NB - 1) | (col_ids == 0) | (col_ids == NB - 1) | (jnp.abs(row_ids - col_ids) <= 1)
    chosen = jnp.any(random_rows[:, :, :, None] == jnp.arange(NB, dtype=jnp.int32)[None, None, None, :], axis=2)
    return fixed_part[None] | chosen

def layer_forward(params, seq_in, allowed_blocks, key_valid):
    gain_one, bias_one, query_weight, query_bias, key_weight, value_weight, value_bias, out_weight, out_bias, gain_two, bias_two, up_weight, up_bias, down_weight, down_bias = params
    normed_one = low(layer_norm(seq_in, gain_one, bias_one))
    queries = low(low_back(matmul(normed_one, query_weight) + query_bias)).reshape(LEN, H, HD)
    key_rows = low(low_back(matmul(normed_one, key_weight))).reshape(LEN, H, HD)
    val_rows = low(low_back(matmul(normed_one, value_weight) + value_bias)).reshape(LEN, H, HD)

    def tile_fn(tile_id):
        tile_q = lax.dynamic_slice_in_dim(queries, tile_id * QB, QB, 0)
        tile_blocks = lax.dynamic_slice_in_dim(allowed_blocks, tile_id * (QB // BLOCK), QB // BLOCK, 1)
        allowed = jnp.repeat(jnp.repeat(tile_blocks, BLOCK, axis=1), BLOCK, axis=2) & key_valid[None, None, :]
        scores = low_back(jnp.einsum('qhd,khd->hqk', tile_q, key_rows, precision=precise) * 0.125)
        scores = jnp.where(allowed, scores, -1e+30)
        row_top = lax.optimization_barrier(jnp.max(scores, axis=-1, keepdims=True))
        raised = jnp.exp(scores - row_top)
        attn_prob = low(raised / lax.optimization_barrier(jnp.sum(raised, axis=-1, keepdims=True)))
        return jnp.einsum('hqk,khd->qhd', attn_prob, val_rows, precision=precise)
    context = lax.map(jax.checkpoint(tile_fn), jnp.arange(LEN // QB, dtype=jnp.int32))
    context = low(low_back(context.reshape(LEN, D)))
    attn_out = low_back(matmul(context, out_weight))
    resid = seq_in + attn_out + out_bias
    normed_two = low(layer_norm(resid, gain_two, bias_two))
    up_proj = low_back(matmul(normed_two, up_weight) + up_bias)
    active = low(jax.nn.gelu(up_proj, approximate=True))
    return resid + matmul(active, down_weight) + down_bias

def reference(inputs, lengths, random_blocks, attn_norm_gain, attn_norm_bias, query_weight, query_bias, key_weight, value_weight, value_bias, out_weight, out_bias, ffn_norm_gain, ffn_norm_bias, up_weight, up_bias, down_weight, down_bias, grad_out):
    weights_in = (attn_norm_gain, attn_norm_bias, query_weight, query_bias, key_weight, value_weight, value_bias, out_weight, out_bias, ffn_norm_gain, ffn_norm_bias, up_weight, up_bias, down_weight, down_bias)
    params = tuple((param_item.astype(jnp.float32) for param_item in weights_in))
    zero_grads = tuple((jnp.zeros_like(param_item) for param_item in params))

    def per_seq(carry, items):
        seq_in, seq_grad, seq_len, seq_rand = items
        allowed_blocks = block_allowed(seq_rand)
        key_valid = jnp.arange(LEN, dtype=jnp.int32) < seq_len

        def forward(param_set, seq_values):
            return layer_forward(param_set, seq_values, allowed_blocks, key_valid)
        result, pullback = jax.vjp(forward, params, seq_in.astype(jnp.float32))
        grad_params, grad_seq = pullback(seq_grad.astype(jnp.float32))
        carry = jax.tree.map(jnp.add, carry, grad_params)
        return (carry, (result.astype(jnp.bfloat16), grad_seq.astype(jnp.bfloat16)))
    stacked = (inputs.reshape(SEQS, LEN, D), grad_out.reshape(SEQS, LEN, D), lengths, random_blocks)
    totals, (seq_outs, seq_grads) = lax.scan(per_seq, zero_grads, stacked)
    return (seq_outs.reshape(TOKENS, D), seq_grads.reshape(TOKENS, D), totals[0], totals[1], totals[2], totals[3], totals[4], totals[5], totals[6], totals[7], totals[8], totals[9], totals[10], totals[11], totals[12], totals[13], totals[14])
```

```python
from functools import partial

import jax
import jax.numpy as jnp
from jax import lax
from jax.experimental import pallas as pl
from jax.experimental.pallas import tpu as pltpu
from jax.sharding import PartitionSpec as P

D = 1024
HD = 64
BLOCK = 64
LEN = 1024
NB = 16
EPS = 1e-05
VMEM_LIMIT = 60 * 1024 * 1024
f32 = jnp.float32
bf16 = jnp.bfloat16
NT = (((1,), (1,)), ((), ()))
NN = (((1,), (0,)), ((), ()))
TN = (((0,), (0,)), ((), ()))


def mm(left, right, dims=NN):
    return lax.dot_general(left, right, dims, preferred_element_type=f32)


def call(kernel, name, grid, in_specs, out_specs, out_shape, scratch=(), flops=0, nbytes=0,
         aliases=None):
    return pl.pallas_call(
        kernel,
        out_shape=out_shape,
        grid_spec=pltpu.PrefetchScalarGridSpec(
            num_scalar_prefetch=1,
            grid=grid,
            in_specs=in_specs,
            out_specs=out_specs,
            scratch_shapes=list(scratch),
        ),
        compiler_params=pltpu.CompilerParams(
            dimension_semantics=("arbitrary",) * len(grid), vmem_limit_bytes=VMEM_LIMIT
        ),
        cost_estimate=pl.CostEstimate(flops=0, bytes_accessed=0, transcendentals=0),
        input_output_aliases=aliases or {},
        name=name,
    )


def sds(shape, dtype):
    return jax.ShapeDtypeStruct(shape, dtype)


def const(shape):
    return pl.BlockSpec(shape, lambda i, z: (0,) * len(shape))


def rows_of(shape):
    return pl.BlockSpec(shape, lambda i, z: (i,) + (0,) * (len(shape) - 1))


def lane_ds(start, size):
    return pl.ds(pl.multiple_of(start, 128), size)


def across(value, mask, size):
    return lax.ppermute(value, "tensor", [(i, i ^ mask) for i in range(size)])


def swap(value, mask, size):
    return lax.ppermute(value, "dp", [(i, i ^ mask) for i in range(size)])


def gather4(value, size):
    far = across(value, 2, size)
    near = across(value, 1, size)
    return [value, near, far, across(far, 1, size)]


def scatter4(slots, size):
    got3 = across(slots[3], 1, size)
    got1 = across(slots[1], 1, size)
    far = (slots[2].astype(f32) + got3.astype(f32)).astype(slots[2].dtype)
    return slots[0], got1, across(far, 2, size)


def sum4(value, size):
    value = value + across(value, 1, size)
    return value + across(value, 2, size)


def stages(size):
    bits = list(range(size.bit_length() - 1))
    return [bits[:1]] + [bits[j:j + 2] for j in range(1, len(bits), 2)]


def digit_of(index, group):
    digit = 0
    for j, bit in enumerate(group):
        digit = digit | (((index >> bit) & 1) << j)
    return digit


def mask_of(k, group):
    return sum(((k >> j) & 1) << bit for j, bit in enumerate(group))


def dp_position(size):
    index = lax.axis_index("dp")
    place = 0
    for group in stages(size):
        place = (place << len(group)) | digit_of(index, group)
    return place.astype(jnp.int32)


def dp_scatter(value, size, axis=0, groups=None):
    index = lax.axis_index("dp")
    for group in stages(size) if groups is None else groups:
        n = 1 << len(group)
        mine = digit_of(index, group)
        rows = value.shape[axis] // n
        take = lambda at: lax.dynamic_slice_in_dim(value, at * rows, rows, axis)
        got = [swap(take(mine ^ k), mask_of(k, group), size) for k in range(1, n)]
        total = take(mine).astype(f32)
        for g in got:
            total = total + g.astype(f32)
        value = total.astype(value.dtype)
    return value


def dp_gather(value, size, groups=None):
    value = value[None]
    for group in (stages(size) if groups is None else groups)[::-1]:
        n = 1 << len(group)
        value = jnp.stack([value] + [swap(value, mask_of(k, group), size) for k in range(1, n)])
        value = value.reshape((-1,) + value.shape[2:])
    return value


def dp_sum_small(value, size):
    for bit in range(size.bit_length() - 1):
        value = value + swap(value, 1 << bit, size)
    return value


def k_place(p_ref, value, *outs):
    w = outs[0].shape[-1]
    for j, out in enumerate(outs):
        out[...] = value[0][..., j * w:(j + 1) * w].astype(out.dtype)


def placed(value, size, dtype, outs=1, axis=0):
    n = value.shape[0]
    block = list(value.shape[1:])
    if block[axis] % 16:
        ordered = value[jnp.bitwise_xor(jnp.arange(n, dtype=jnp.int32), dp_position(size))]
        ordered = jnp.moveaxis(ordered, 0, axis)
        shape = block[:axis] + [n * block[axis]] + block[axis + 1:]
        return jnp.split(ordered.reshape(shape).astype(dtype), outs, axis=-1)
    block[-1] //= outs
    whole = list(block)
    whole[axis] *= n
    index = lambda i, p: tuple(
        jnp.bitwise_xor(i, p[0]) if d == axis else 0 for d in range(len(block)))
    return call(
        k_place, "place", (n,),
        [pl.BlockSpec((1,) + tuple(value.shape[1:]), lambda i, p: (i,) + (0,) * len(block))],
        [pl.BlockSpec(tuple(block), index)] * outs, [sds(tuple(whole), dtype)] * outs,
        nbytes=6 * value.size,
    )(dp_position(size).reshape(1), value)


def k_place_two(p_ref, one, two, up, down):
    first = p_ref[1] == 0
    up[...] = jnp.where(first, one[0], two[0]).astype(f32)
    down[...] = jnp.where(first, two[0], one[0]).astype(f32)


def dp_sum_two(up, down, size):
    groups = stages(size)
    side = digit_of(lax.axis_index("dp"), groups[0])
    sent = jnp.where(side == 0, down, up)
    kept = jnp.where(side == 0, up, down)
    part = (kept.astype(f32) + swap(sent, 1, size).astype(f32)).astype(bf16)
    part = dp_scatter(part, size, groups=groups[1:])
    one = dp_gather(part, size, groups=groups[1:])
    return one


def dp_sum_two_end(one, size):
    groups = stages(size)
    side = digit_of(lax.axis_index("dp"), groups[0])
    two = swap(one, 1, size)
    n, rows, cols = one.shape
    block = pl.BlockSpec((1, rows, cols), lambda i, p: (i, 0, 0))
    place = pl.BlockSpec((rows, cols), lambda i, p: (jnp.bitwise_xor(i, p[0] % n), 0))
    return call(
        k_place_two, "place_two", (n,), [block, block], [place, place],
        [sds((n * rows, cols), f32)] * 2, nbytes=12 * n * rows * cols,
    )(jnp.stack([dp_position(size), side.astype(jnp.int32)]), one, two)


def norm_stats(x):
    m = jnp.mean(x, axis=-1, keepdims=True)
    c = x - m
    r = lax.rsqrt(jnp.mean(c * c, axis=-1, keepdims=True) + EPS)
    return m, c, r


def k_qkv(z_ref, x0, x1, x2, x3, s0, s1, s2, s3, wq, wk, wv,
          x_out, n_out, q_out, k_out, v_out, nl_out, r_out, g_out):
    z = z_ref[0]
    w = x0.shape[1]
    for r, (xb, s) in enumerate(((x0, s0), (x1, s1), (x2, s2), (x3, s3))):
        at = lane_ds(jnp.bitwise_xor(z, r) * w, w)
        x_out[:, at] = xb[...]
        g_out[:, at] = s[...].astype(f32)
    m, c, r = norm_stats(x_out[...].astype(f32))
    n = (c * r * g_out[0:1, :] + g_out[1:2, :]).astype(bf16)
    n_out[...] = n
    nl_out[...] = (x0[...].astype(f32) - m) * r
    r_out[...] = jnp.broadcast_to(r, r_out.shape)
    small = s0[...].astype(f32)
    q_out[...] = ((mm(n, wq[...]) + small[5:6, :]).astype(bf16) * 0.125).astype(bf16)
    k_out[...] = mm(n, wk[...]).astype(bf16)
    v_out[...] = (mm(n, wv[...]) + small[6:7, :]).astype(bf16)


def low_lanes(shape):
    return lax.broadcasted_iota(jnp.int32, shape, len(shape) - 1) < HD


def k_attend(z_ref, q, k, v, bias, ctx_out, p_out):
    rows = q.shape[0]
    nblk = rows // BLOCK
    low = low_lanes((rows, 2 * HD))
    heads = q.shape[1] // HD
    for pair in range(heads // 2):
        lanes = slice(pair * 2 * HD, (pair + 1) * 2 * HD)
        qp = q[:, lanes]
        kp = k[:, lanes]
        vp = v[:, lanes]
        parts = []
        for side in range(2):
            h = pair * 2 + side
            qm = jnp.where(low if side == 0 else ~low, qp, jnp.zeros_like(qp))
            s = mm(qm, kp, NT)
            pieces = []
            for b in range(nblk):
                sb = s[b * BLOCK:(b + 1) * BLOCK] + bias[b * heads + h:b * heads + h + 1, :]
                top = jnp.max(sb, axis=-1, keepdims=True)
                e = jnp.exp(sb - top)
                total = jnp.sum(e, axis=-1, keepdims=True)
                pieces.append((e * (1.0 / total)).astype(bf16))
            p = jnp.concatenate(pieces, 0)
            p_out[h] = p
            parts.append(mm(p, vp))
        ctx_out[:, lanes] = jnp.where(low, parts[0], parts[1]).astype(bf16)


def k_ffn(base, z_ref, c0, c1, c2, c3, g0, g1, g2, g3, x, gains, wo0, wo, wu, ub, wd, *rest):
    (go_out, res_out, n_out, act_out, gup_out, d0, d1, d2, d3,
     h0, h1, h2, h3, sums_out) = rest[-14:]
    i = pl.program_id(0)
    z = z_ref[0]
    w = c0.shape[1]
    attn = mm(c0[...], wo0[...])
    for r, c in enumerate((c1, c2, c3)):
        attn = attn + mm(c[...], wo[r])
    for r, g in enumerate((g0, g1, g2, g3)):
        go_out[:, lane_ds(jnp.bitwise_xor(z, r) * w, w)] = g[...]
    resid = x[...].astype(f32) + attn + gains[2:3, :]
    res_out[...] = resid
    m, c, r = norm_stats(resid)
    n = (c * r * gains[3:4, :] + gains[4:5, :]).astype(bf16)
    n_out[...] = n
    u = mm(n, wu[...]) + ub[...].astype(f32)
    uu = u * u
    t = jnp.tanh(0.7978845608028654 * u * (1.0 + 0.044715 * uu))
    half = 0.5 * (1.0 + t)
    act = (u * half).astype(bf16)
    slope = half + 0.5 * u * (1.0 - t * t) * (0.7978845608028654 * (1.0 + 0.134145 * uu))
    act_out[...] = act
    gup = (mm(go_out[...], wd[...], NT) * slope).astype(bf16)
    gup_out[...] = gup
    gnt = mm(gup, wu[...], NT).astype(bf16)
    seg = h0.shape[0]
    per = gnt.shape[0] // seg
    for s in range(per):
        for r, h in enumerate((h0, h1, h2, h3)):
            @pl.when(jnp.bitwise_xor(i * per + s, z) == r)
            def _():
                h[...] = gnt[s * seg:(s + 1) * seg]

    own = lane_ds(z * w, w)
    d0[...] = res_out[:, own] + mm(act, wd[:, own]) + gains[7:8, own]
    for r, d in ((1, d1), (2, d2), (3, d3)):
        d[...] = mm(act, wd[:, lane_ds(jnp.bitwise_xor(z, r) * w, w)]).astype(bf16)

    @pl.when(i == 0)
    def _():
        sums_out[...] = jnp.zeros_like(sums_out)

    sums_out[0:1, :] += jnp.sum(gup.astype(f32), axis=0, keepdims=True)
    sums_out[1:2, 0:w] += jnp.sum(g0[...].astype(f32), axis=0, keepdims=True)


def k_norm_two(z_ref, h0, h1, h2, resid, go, gains, wo0, wo, gr_out, gb_out, o0, o1, o2, o3, sums_out):
    gnt = h0[...].astype(f32) + h1[...].astype(f32) + h2[...].astype(f32)
    m, c, r = norm_stats(resid[...])
    n = c * r
    e = gnt * gains[3:4, :]
    me = jnp.mean(e, axis=-1, keepdims=True)
    mn = jnp.mean(e * n, axis=-1, keepdims=True)
    gres = go[...].astype(f32) + r * (e - me - n * mn)
    gr_out[...] = gres
    gb = gres.astype(bf16)
    gb_out[...] = gb
    sums_out[...] = jnp.zeros_like(sums_out)
    sums_out[0:1, :] = jnp.sum(gnt * n, axis=0, keepdims=True)
    sums_out[1:2, :] = jnp.sum(gnt, axis=0, keepdims=True)
    sums_out[2:3, :] = jnp.sum(gres, axis=0, keepdims=True)
    o0[...] = mm(gb, wo0[...], NT).astype(bf16)
    for k, o in enumerate((o1, o2, o3)):
        o[...] = mm(gb, wo[k], NT).astype(bf16)


def k_dw_out(z_ref, a0, a1, a2, a3, b0, b1, b2, b3, gb_a, gb_b, out):
    gb = jnp.concatenate([gb_a[...], gb_b[...]], axis=0)
    for r, (a, b) in enumerate(((a0, b0), (a1, b1), (a2, b2), (a3, b3))):
        out[r] = mm(jnp.concatenate([a[...], b[...]], axis=0), gb, TN).astype(bf16)


def k_dw_qkv(z_ref, n, gq, gk, gv, out):
    w = gq.shape[1]
    nv = n[...]
    for j, g in enumerate((gq, gk, gv)):
        out[:, j * w:(j + 1) * w] = mm(nv, g[...], TN).astype(bf16)


def k_attend_back(z_ref, q, k, v, p_a, p_b, ctx_a, ctx_b, e0, e1, e2, e3, f0, f1, f2, f3,
                  gq_out, gk_out, gv_out, sums_out, gc, gs, cx):
    z = z_ref[0]
    rows = e0.shape[0]
    total = q.shape[0]
    half = total // 2
    for h, es in enumerate(((e0, e1, e2, e3), (f0, f1, f2, f3))):
        for j, e in enumerate(es):
            at = h * half + jnp.bitwise_xor(z, j) * rows
            gc[pl.ds(pl.multiple_of(at, rows), rows), :] = e[...]
    cx[:half] = ctx_a[...]
    cx[half:] = ctx_b[...]
    low = low_lanes((total, 2 * HD))
    qp, kp, vp = q[...], k[...], v[...]
    gcv = gc[...]
    prod = gcv.astype(f32) * cx[...].astype(f32)
    gq, gk, gv = [], [], []
    for side in range(2):
        pick = low if side == 0 else ~low
        delta = jnp.sum(jnp.where(pick, prod, 0.0), axis=-1, keepdims=True)
        gm = jnp.where(pick, gcv, jnp.zeros_like(gcv))
        tile = 256
        for t in range(total // tile):
            at = slice(t * tile, (t + 1) * tile)
            gp = mm(gm[at], vp, NT)
            p = p_a if t * tile < half else p_b
            pt = p[side, t * tile % half:t * tile % half + tile, :].astype(f32)
            gs[at, :] = (pt * (gp - delta[at])).astype(bf16)
        gsv = gs[...]
        gq.append(mm(gsv, kp))
        gk.append(mm(qp, gsv, TN))
        gv.append(mm(gcv[:half], p_a[side], TN) + mm(gcv[half:], p_b[side], TN))
    gqv = (jnp.where(low, gq[0], gq[1]) * 0.125).astype(bf16)
    gq_out[...] = gqv
    top = lax.broadcasted_iota(jnp.int32, gk[0].shape, 0) < HD
    gk_out[...] = jnp.where(top, gk[0], gk[1]).T.astype(bf16)
    gvv = jnp.where(top, gv[0], gv[1]).T.astype(bf16)
    gv_out[...] = gvv
    sums_out[...] = jnp.zeros_like(sums_out)
    sums_out[0:1, :] = jnp.sum(gqv.astype(f32), axis=0, keepdims=True)
    sums_out[1:2, :] = jnp.sum(gvv.astype(f32), axis=0, keepdims=True)


def k_norm_one(z_ref, gq, gk, gv, wq, wk, wv, x, gains, gres_a, gres_b, o0, o1, o2, o3,
               stats_out, sums_out, scr):
    i = pl.program_id(0)
    z = z_ref[0]
    w = gq.shape[1]
    gn = mm(gq[...], wq[...], NT) + mm(gk[...], wk[...], NT) + mm(gv[...], wv[...], NT)
    m, c, r = norm_stats(x[...].astype(f32))
    n = c * r
    e = gn * gains[0:1, :]
    en = e * n
    se = jnp.sum(e, axis=-1, keepdims=True)
    de = jnp.sum(en, axis=-1, keepdims=True)
    lane = lax.broadcasted_iota(jnp.int32, (gn.shape[0], 128), 1)
    cols = jnp.where(lane == 0, se, jnp.where(lane == 1, de, 0.0))
    stats_out[...] = cols.T[0:8, :]
    scr[...] = r * e
    seg = gres_a.shape[0]
    rows = gn.shape[0]
    per_half = pl.num_programs(0) // 2
    for h, gres in enumerate((gres_a, gres_b)):
        @pl.when(i == h * per_half + (z * seg) // rows)
        def _():
            scr[pl.ds(pl.multiple_of((z * seg) % rows, seg), seg), :] += gres[...]

    for r, o in enumerate((o0, o1, o2, o3)):
        o[...] = scr[:, lane_ds(jnp.bitwise_xor(z, r) * w, w)].astype(bf16)

    @pl.when(i == 0)
    def _():
        sums_out[...] = jnp.zeros_like(sums_out)

    sums_out[0:1, :] += jnp.sum(gn * n, axis=0, keepdims=True)
    sums_out[1:2, :] += jnp.sum(gn, axis=0, keepdims=True)


def k_final(z_ref, t0, t1, t2, stats, nl, r, out):
    total = t0[...].astype(f32) + t1[...].astype(f32) + t2[...].astype(f32)
    cols = jnp.concatenate([stats[...]] * 16, 0).T * (1.0 / D)
    out[...] = (total - r[:, 0:1] * (cols[:, 0:1] + nl[...] * cols[:, 1:2])).astype(bf16)


def mask_bias(random_rows, length):
    heads = random_rows.shape[0]
    rows = jnp.arange(NB, dtype=jnp.int32)[:, None]
    cols = jnp.arange(NB, dtype=jnp.int32)[None, :]
    fixed = (
        (rows == 0) | (rows == NB - 1) | (cols == 0) | (cols == NB - 1)
        | (jnp.abs(rows - cols) <= 1)
    )
    chosen = jnp.any(random_rows[:, :, :, None] == cols[0][None, None, None, :], axis=2)
    allowed = jnp.transpose(fixed[None] | chosen, (1, 0, 2)).reshape(NB * heads, NB)
    valid = jnp.arange(LEN, dtype=jnp.int32) < length
    return jnp.where(jnp.repeat(allowed, BLOCK, axis=1) & valid[None, :], 0.0, -1e30).astype(f32)


def make_shards(dp, tp):
    def shards(inputs, lengths, random_blocks, attn_norm_gain, attn_norm_bias, query_weight,
               query_bias, key_weight, value_weight, value_bias, out_weight, out_bias,
               ffn_norm_gain, ffn_norm_bias, up_weight, up_bias, down_weight, down_bias, grad_out):
        tokens, w = inputs.shape
        ff = up_weight.shape[1]
        heads = w // HD
        half = tokens // 2
        quarter = tokens // tp
        tile = 256
        zi = lax.axis_index("tensor")
        z = zi.astype(jnp.int32).reshape(1)
        d_i = lax.axis_index("dp")

        seg = half // tp
        here_dp = dp_position(dp)
        part_rows = w // dp
        pack = D // dp
        zero = jnp.zeros((1, w), bf16)
        small = jnp.concatenate(
            [v.reshape(1, w) for v in (attn_norm_gain, attn_norm_bias, out_bias, ffn_norm_gain,
                                       ffn_norm_bias, query_bias, value_bias, down_bias)]
            + [zero] * 8, 0)
        wo_part = lax.dynamic_slice_in_dim(out_weight, here_dp * part_rows, part_rows, 0)
        first = jnp.concatenate([inputs, small, wo_part.reshape(pack, w)], 0)
        slots = gather4(first, tp)

        bias = mask_bias(random_blocks[0], lengths[0])

        tw, td = rows_of((tile, w)), rows_of((tile, D))
        small_at = pl.BlockSpec((16, w), lambda i, z: (tokens // 16, 0))
        x_full, n_one, q, k, v, n_loc, r_one, gains = call(
            k_qkv, "qkv", (tokens // tile,),
            [tw] * 4 + [small_at] * 4 + [const((D, w))] * 3,
            [td, td, tw, tw, tw, tw, rows_of((tile, 128)), const((16, D))],
            [sds((tokens, D), bf16), sds((tokens, D), bf16), sds((tokens, w), bf16),
             sds((tokens, w), bf16), sds((tokens, w), bf16), sds((tokens, w), f32),
             sds((tokens, 128), f32), sds((16, D), f32)],
            flops=2 * tokens * D * 3 * w, nbytes=12 << 20,
        )(z, *slots, *slots, query_weight, key_weight, value_weight)

        go_in, _ = lax.optimization_barrier((grad_out, slots[3]))
        gos = gather4(go_in, tp)

        nblk = tile // BLOCK
        att = []
        for h in range(2):
            steps = half // tile
            base = h * steps
            att.append(call(
                k_attend, "attend", (steps,),
                [pl.BlockSpec((tile, w), lambda i, z, base=base: (i + base, 0)),
                 const((tokens, w)), const((tokens, w)),
                 pl.BlockSpec((nblk * heads, LEN), lambda i, z, base=base: (i + base, 0))],
                [tw, pl.BlockSpec((heads, tile, LEN), lambda i, z: (0, i, 0))],
                [sds((half, w), bf16), sds((heads, half, LEN), bf16)],
                flops=2 * half * LEN * 128 * heads * 2, nbytes=8 << 20,
            )(z, q, k, v, bias))
        ctxs = [gather4(att[h][0], tp) for h in range(2)]

        wo_in = jnp.stack([s[tokens + 16:].reshape(part_rows, D) for s in slots[1:]])
        wo_in, _ = lax.optimization_barrier((wo_in, att[1][0]))
        (wo_rest,) = placed(dp_gather(wo_in, dp), dp, bf16, axis=1)

        ffn = []
        carried = []
        for h in range(2):
            steps = half // tile
            base = h * steps
            here = lambda i, z, base=base: (i + base, 0)
            hw, hd, hf = (pl.BlockSpec((tile, n), here) for n in (w, D, ff))
            n_in = 18
            out = call(
                partial(k_ffn, base), "ffn", (steps,),
                [tw] * 4 + [hw] * 4 + [hd, const((16, D)), const((w, D)), const((tp - 1, w, D)),
                                       const((D, ff)), const((1, ff)), const((ff, D))]
                + [pl.BlockSpec(memory_space=pl.ANY)] * len(carried),
                [hd, hd, hd, hf, hf, hw, hw, hw, hw] + [const((seg, D))] * 4 + [const((8, ff))],
                [sds((tokens, D), bf16), sds((tokens, D), f32), sds((tokens, D), bf16),
                 sds((tokens, ff), bf16), sds((tokens, ff), bf16), sds((tokens, w), f32)]
                + [sds((tokens, w), bf16)] * 3 + [sds((seg, D), bf16)] * 4 + [sds((8, ff), f32)],
                flops=2 * half * D * ff * 5, nbytes=24 << 20,
                aliases={16 + j: j for j in range(len(carried))},
            )(z, *ctxs[h], *gos, x_full, gains, out_weight, wo_rest, up_weight,
              up_bias.reshape(1, ff), down_weight, *carried)
            carried = out[:9]
            ffn.append(out)
        go_full, res_full, n_two, act, gup, d0, d1, d2, d3 = carried

        two = []
        for h in range(2):
            h0, h1, h2 = scatter4(ffn[h][9:13], tp)
            at_z = pl.BlockSpec((seg, D), lambda i, z, h=h: (h * tp + z[0], 0))
            two.append(call(
                k_norm_two, "norm_two", (1,),
                [const((seg, D))] * 3 + [at_z, at_z, const((16, D)), const((w, D)),
                                         const((tp - 1, w, D))],
                [const((seg, D)), const((seg, D))] + [const((seg, w))] * 4 + [const((8, D))],
                [sds((seg, D), f32), sds((seg, D), bf16)] + [sds((seg, w), bf16)] * 4
                + [sds((8, D), f32)],
                flops=2 * seg * D * D, nbytes=10 << 20,
            )(z, h0, h1, h2, res_full, go_full, gains, out_weight, wo_rest))
        g_ctx = [[two[h][2]] + [across(two[h][2 + r], r, tp) for r in range(1, tp)]
                 for h in range(2)]

        (d1, d2, d3), _ = lax.optimization_barrier(((d1, d2, d3), g_ctx[1]))
        outputs = sum(t.astype(f32) for t in scatter4([d0, d1, d2, d3], tp)).astype(bf16)

        pair = pl.BlockSpec((tokens, 2 * HD), lambda i, z: (0, i))
        pairh = pl.BlockSpec((half, 2 * HD), lambda i, z: (0, i))
        probs = pl.BlockSpec((2, half, LEN), lambda i, z: (i, 0, 0))
        gq, gk, gv, sums_qkv = call(
            k_attend_back, "attend_back", (heads // 2,),
            [pair, pair, pair, probs, probs, pairh, pairh]
            + [pl.BlockSpec((seg, 2 * HD), lambda i, z: (0, i))] * 8,
            [pair, pair, pair, pl.BlockSpec((8, 2 * HD), lambda i, z: (0, i))],
            [sds((tokens, w), bf16)] * 3 + [sds((8, w), f32)],
            scratch=[pltpu.VMEM((tokens, 2 * HD), bf16), pltpu.VMEM((tokens, LEN), bf16),
                     pltpu.VMEM((tokens, 2 * HD), bf16)],
            flops=2 * tokens * LEN * 128 * heads * 4, nbytes=12 << 20,
        )(z, q, k, v, att[0][1], att[1][1], att[0][0], att[1][0], *g_ctx[0], *g_ctx[1])

        *contrib, stats, sums_one = call(
            k_norm_one, "norm_one", (tokens // tile,),
            [tw] * 3 + [const((D, w))] * 3 + [td, const((16, D)), const((seg, D)), const((seg, D))],
            [tw] * 4 + [pl.BlockSpec((8, tile), lambda i, z: (0, i)), const((8, D))],
            [sds((tokens, w), bf16)] * 4 + [sds((8, tokens), f32), sds((8, D), f32)],
            scratch=[pltpu.VMEM((tile, D), f32)],
            flops=2 * tokens * D * 3 * w, nbytes=12 << 20,
        )(z, gq, gk, gv, query_weight, key_weight, value_weight, x_full, gains, two[0][0], two[1][0])

        totals = scatter4(contrib, tp)
        sums_two = two[0][6] + two[1][6]
        mix = jnp.concatenate([stats[0:2], sums_one[0:2], sums_two[0:3], jnp.zeros((1, D), f32)], 0)
        mix = sum4(mix, tp)
        grad_inputs = call(
            k_final, "final", (tokens // tile,),
            [tw] * 3 + [pl.BlockSpec((8, tile), lambda i, z: (0, i)), tw, rows_of((tile, 128))],
            tw, sds((tokens, w), bf16), flops=tokens * w * 8, nbytes=5 << 20,
        )(z, *totals, mix, n_loc, r_one)

        dw_up = mm(n_two, gup, TN).astype(bf16)
        dw_down = mm(act, go_full, TN).astype(bf16)
        g_up, g_down = dp_sum_two_end(dp_sum_two(dw_up, dw_down, dp), dp)

        seg_z = pl.BlockSpec((seg, w), lambda i, z: (z[0], 0))
        dw_out = call(
            k_dw_out, "dw_out", (1,), [seg_z] * 8 + [const((seg, D))] * 2, const((tp, w, D)),
            sds((tp, w, D), bf16), flops=2 * 2 * seg * D * D, nbytes=5 << 20,
        )(z, *ctxs[0], *ctxs[1], two[0][1], two[1][1])
        piece = dp_scatter(dw_out, dp, axis=1)
        own = piece[0].astype(f32)
        for r in range(1, tp):
            own = own + across(piece[r], r, tp).astype(f32)
        (g_out_w,) = placed(dp_gather(own.astype(bf16), dp), dp, f32)

        dw_qkv = call(
            k_dw_qkv, "dw_qkv", (D // tile,),
            [pl.BlockSpec((tokens, tile), lambda i, z: (0, i))] + [const((tokens, w))] * 3,
            rows_of((tile, 3 * w)), sds((D, 3 * w), bf16), flops=2 * tokens * D * 3 * w, nbytes=5 << 20,
        )(z, n_one, gq, gk, gv)
        g_q, g_k, g_v = placed(dp_gather(dp_scatter(dw_qkv, dp), dp), dp, f32, outs=3)

        mine = lax.dynamic_slice_in_dim(mix, zi * w, w, 1)
        up_sum = ffn[0][13] + ffn[1][13]
        vec = jnp.concatenate([
            mine[2], mine[3], mine[4], mine[5], mine[6], sums_qkv[0], sums_qkv[1],
            up_sum[1, :w], up_sum[0],
        ]).reshape(-1, 128)
        vec = dp_sum_small(vec, dp).reshape(-1)
        pieces = [vec[j * w:(j + 1) * w] for j in range(8)]
        g_up_b = vec[8 * w:]
        return (outputs, grad_inputs, pieces[0], pieces[1], g_q, pieces[5], g_k, g_v, pieces[6],
                g_out_w, pieces[4], pieces[2], pieces[3], g_up, g_up_b, g_down, pieces[7])

    return shards


def solution(mesh):
    return jax.shard_map(
        make_shards(mesh.shape["dp"], mesh.shape["tensor"]),
        mesh=mesh,
        in_specs=(
            P("dp", "tensor"), P("dp"), P("dp", "tensor", None, None), P("tensor"), P("tensor"),
            P(None, "tensor"), P("tensor"), P(None, "tensor"), P(None, "tensor"), P("tensor"),
            P("tensor", None), P("tensor"), P("tensor"), P("tensor"), P(None, "tensor"),
            P("tensor"), P("tensor", None), P("tensor"), P("dp", "tensor"),
        ),
        out_specs=(
            P("dp", "tensor"), P("dp", "tensor"), P("tensor"), P("tensor"), P(None, "tensor"),
            P("tensor"), P(None, "tensor"), P(None, "tensor"), P("tensor"), P("tensor", None),
            P("tensor"), P("tensor"), P("tensor"), P(None, "tensor"), P("tensor"),
            P("tensor", None), P("tensor"),
        ),
        check_vma=False,
    )
```

```python
from functools import partial

import jax
import jax.numpy as jnp
from jax import lax
from jax.experimental import pallas as pl
from jax.experimental.pallas import tpu as pltpu
from jax.sharding import PartitionSpec as P

D = 1024
HD = 64
BLOCK = 64
LEN = 1024
NB = 16
EPS = 1e-05
VMEM_LIMIT = 60 * 1024 * 1024
f32 = jnp.float32
bf16 = jnp.bfloat16
NT = (((1,), (1,)), ((), ()))
NN = (((1,), (0,)), ((), ()))
TN = (((0,), (0,)), ((), ()))


def mm(left, right, dims=NN):
    return lax.dot_general(left, right, dims, preferred_element_type=f32)


def call(kernel, name, grid, in_specs, out_specs, out_shape, scratch=(), flops=0, nbytes=0,
         aliases=None):
    return pl.pallas_call(
        kernel,
        out_shape=out_shape,
        grid_spec=pltpu.PrefetchScalarGridSpec(
            num_scalar_prefetch=1,
            grid=grid,
            in_specs=in_specs,
            out_specs=out_specs,
            scratch_shapes=list(scratch),
        ),
        compiler_params=pltpu.CompilerParams(
            dimension_semantics=("arbitrary",) * len(grid), vmem_limit_bytes=VMEM_LIMIT
        ),
        cost_estimate=pl.CostEstimate(flops=0, bytes_accessed=0, transcendentals=0),
        input_output_aliases=aliases or {},
        name=name,
    )


def sds(shape, dtype):
    return jax.ShapeDtypeStruct(shape, dtype)


def const(shape):
    return pl.BlockSpec(shape, lambda i, z: (0,) * len(shape))


def rows_of(shape):
    return pl.BlockSpec(shape, lambda i, z: (i,) + (0,) * (len(shape) - 1))


def lane_ds(start, size):
    return pl.ds(pl.multiple_of(start, 128), size)


def after(value, *others):
    return lax.optimization_barrier((value, others))[0]


def across(value, mask, size):
    return lax.ppermute(value, "tensor", [(i, i ^ mask) for i in range(size)])


def swap(value, mask, size):
    return lax.ppermute(value, "dp", [(i, i ^ mask) for i in range(size)])


def gather4(value, size):
    far = across(value, 2, size)
    near = across(value, 1, size)
    return [value, near, far, across(far, 1, size)]


def scatter4(slots, size):
    got3 = across(slots[3], 1, size)
    got1 = across(slots[1], 1, size)
    far = (slots[2].astype(f32) + got3.astype(f32)).astype(slots[2].dtype)
    return slots[0], got1, across(far, 2, size)


def sum4(value, size):
    value = value + across(value, 1, size)
    return value + across(value, 2, size)


def stages(size):
    bits = list(range(size.bit_length() - 1))
    return [bits[:1]] + [bits[j:j + 2] for j in range(1, len(bits), 2)]


def digit_of(index, group):
    digit = 0
    for j, bit in enumerate(group):
        digit = digit | (((index >> bit) & 1) << j)
    return digit


def mask_of(k, group):
    return sum(((k >> j) & 1) << bit for j, bit in enumerate(group))


def dp_position(size):
    index = lax.axis_index("dp")
    place = 0
    for group in stages(size):
        place = (place << len(group)) | digit_of(index, group)
    return place.astype(jnp.int32)


def dp_scatter(value, size, axis=0, groups=None):
    index = lax.axis_index("dp")
    for group in stages(size) if groups is None else groups:
        n = 1 << len(group)
        mine = digit_of(index, group)
        rows = value.shape[axis] // n
        take = lambda at: lax.dynamic_slice_in_dim(value, at * rows, rows, axis)
        got = [swap(take(mine ^ k), mask_of(k, group), size) for k in range(1, n)]
        total = take(mine).astype(f32)
        for g in got:
            total = total + g.astype(f32)
        value = total.astype(value.dtype)
    return value


def dp_gather_near(value, size):
    value = value[None]
    for group in stages(size)[1:][::-1]:
        n = 1 << len(group)
        value = jnp.stack([value] + [swap(value, mask_of(k, group), size) for k in range(1, n)])
        value = value.reshape((-1,) + value.shape[2:])
    return value


def dp_gather(value, size):
    one = dp_gather_near(value, size)
    return one, swap(one, 1, size)


def dp_sum_small(value, size):
    for bit in range(size.bit_length() - 1):
        value = value + swap(value, 1 << bit, size)
    return value


def k_assemble(axis, p_ref, one, two, *outs):
    n, rows = one.shape[0], one.shape[1 + axis]
    w = outs[0].shape[-1]
    for flip, value in ((0, one), (1, two)):
        for k in range(n):
            at = pl.ds(pl.multiple_of(jnp.bitwise_xor(p_ref[0], flip * n + k) * rows, rows), rows)
            block = value[k]
            for j, out in enumerate(outs):
                out[(slice(None),) * axis + (at,)] = block[..., j * w:(j + 1) * w].astype(out.dtype)


def assemble(pieces, size, dtype, outs=1, axis=0):
    one, two = pieces
    n = 2 * one.shape[0]
    block = list(one.shape[1:])
    if block[axis] % 16:
        order = jnp.bitwise_xor(jnp.arange(n, dtype=jnp.int32), dp_position(size))
        ordered = jnp.moveaxis(jnp.concatenate([one, two], 0)[order], 0, axis)
        shape = block[:axis] + [n * block[axis]] + block[axis + 1:]
        return jnp.split(ordered.reshape(shape).astype(dtype), outs, axis=-1)
    whole = list(block)
    whole[-1] //= outs
    whole[axis] *= n
    return call(
        partial(k_assemble, axis), "assemble", (1,), [const(one.shape)] * 2,
        [const(tuple(whole))] * outs, [sds(tuple(whole), dtype)] * outs, nbytes=12 * one.size,
    )(dp_position(size).reshape(1), one, two)


def norm_stats(x):
    m = jnp.mean(x, axis=-1, keepdims=True)
    c = x - m
    r = lax.rsqrt(jnp.mean(c * c, axis=-1, keepdims=True) + EPS)
    return m, c, r


def k_qkv(z_ref, x0, x1, x2, x3, s0, s1, s2, s3, wqkv,
          x_out, n_out, q_out, k_out, v_out, nl_out, r_out, g_out):
    z = z_ref[0]
    w = x0.shape[1]
    for r, (xb, s) in enumerate(((x0, s0), (x1, s1), (x2, s2), (x3, s3))):
        at = lane_ds(jnp.bitwise_xor(z, r) * w, w)
        x_out[:, at] = xb[...]
        g_out[:, at] = s[0:16, :].astype(f32)
    m, c, r = norm_stats(x_out[...].astype(f32))
    n = (c * r * g_out[0:1, :] + g_out[1:2, :]).astype(bf16)
    n_out[...] = n
    nl_out[...] = (x0[...].astype(f32) - m) * r
    r_out[...] = jnp.broadcast_to(r, r_out.shape)
    small = s0[0:16, :].astype(f32)
    full = mm(n, wqkv[...])
    q_out[...] = ((full[:, :w] + small[5:6, :]).astype(bf16) * 0.125).astype(bf16)
    k_out[...] = full[:, w:2 * w].astype(bf16)
    v_out[...] = (full[:, 2 * w:] + small[6:7, :]).astype(bf16)


def low_lanes(shape):
    return lax.broadcasted_iota(jnp.int32, shape, len(shape) - 1) < HD


def k_attend(z_ref, q, k, v, bias, ctx_out, p_out):
    rows = q.shape[0]
    nblk = rows // BLOCK
    low = low_lanes((rows, 2 * HD))
    heads = q.shape[1] // HD
    for pair in range(heads // 2):
        lanes = slice(pair * 2 * HD, (pair + 1) * 2 * HD)
        qp = q[:, lanes]
        kp = k[:, lanes]
        vp = v[:, lanes]
        parts = []
        for side in range(2):
            h = pair * 2 + side
            qm = jnp.where(low if side == 0 else ~low, qp, jnp.zeros_like(qp))
            s = mm(qm, kp, NT)
            pieces = []
            for b in range(nblk):
                sb = s[b * BLOCK:(b + 1) * BLOCK] + bias[b * heads + h:b * heads + h + 1, :]
                top = jnp.max(sb, axis=-1, keepdims=True)
                e = jnp.exp(sb - top)
                total = jnp.sum(e, axis=-1, keepdims=True)
                pieces.append((e * (1.0 / total)).astype(bf16))
            p = jnp.concatenate(pieces, 0)
            p_out[h] = p
            parts.append(mm(p, vp))
        ctx_out[:, lanes] = jnp.where(low, parts[0], parts[1]).astype(bf16)


def k_ffn(base, z_ref, c0, c1, c2, c3, gs, g_own, x, gains, wo0, wo, wu, ub, wd, *rest):
    (go_out, res_out, n_out, act_out, gup_out, d0, d1, d2, d3,
     h0, h1, h2, h3, sums_out) = rest[-14:]
    i = pl.program_id(0)
    z = z_ref[0]
    w = c0.shape[1]
    attn = mm(c0[...], wo0[...])
    for r, c in enumerate((c1, c2, c3)):
        attn = attn + mm(c[...], wo[r])
    for j in range(gs.shape[0]):
        go_out[:, j * w:(j + 1) * w] = gs[j]
    resid = x[...].astype(f32) + attn + gains[2:3, :]
    res_out[...] = resid
    m, c, r = norm_stats(resid)
    n = (c * r * gains[3:4, :] + gains[4:5, :]).astype(bf16)
    n_out[...] = n
    u = mm(n, wu[...]) + ub[...].astype(f32)
    uu = u * u
    t = jnp.tanh(0.7978845608028654 * u * (1.0 + 0.044715 * uu))
    half = 0.5 * (1.0 + t)
    act = (u * half).astype(bf16)
    slope = half + 0.5 * u * (1.0 - t * t) * (0.7978845608028654 * (1.0 + 0.134145 * uu))
    act_out[...] = act
    gup = (mm(go_out[...], wd[...], NT) * slope).astype(bf16)
    gup_out[...] = gup
    gnt = mm(gup, wu[...], NT).astype(bf16)
    seg = h0.shape[0]
    per = gnt.shape[0] // seg
    for s in range(per):
        for r, h in enumerate((h0, h1, h2, h3)):
            @pl.when(jnp.bitwise_xor(i * per + s, z) == r)
            def _():
                h[...] = gnt[s * seg:(s + 1) * seg]

    own = lane_ds(z * w, w)
    d0[...] = res_out[:, own] + mm(act, wd[:, own]) + gains[7:8, own]
    for r, d in ((1, d1), (2, d2), (3, d3)):
        d[...] = mm(act, wd[:, lane_ds(jnp.bitwise_xor(z, r) * w, w)]).astype(bf16)

    @pl.when(i == 0)
    def _():
        sums_out[...] = jnp.zeros_like(sums_out)

    sums_out[0:1, :] += jnp.sum(gup.astype(f32), axis=0, keepdims=True)
    sums_out[1:2, 0:w] += jnp.sum(g_own[...].astype(f32), axis=0, keepdims=True)


def k_norm_two(z_ref, h0, h1, h2, resid, go, gains, wo0, wo, gr_out, gb_out, o0, o1, o2, o3, sums_out):
    gnt = h0[...].astype(f32) + h1[...].astype(f32) + h2[...].astype(f32)
    m, c, r = norm_stats(resid[...])
    n = c * r
    e = gnt * gains[3:4, :]
    me = jnp.mean(e, axis=-1, keepdims=True)
    mn = jnp.mean(e * n, axis=-1, keepdims=True)
    gres = go[...].astype(f32) + r * (e - me - n * mn)
    gr_out[...] = gres
    gb = gres.astype(bf16)
    gb_out[...] = gb
    sums_out[...] = jnp.zeros_like(sums_out)
    sums_out[0:1, :] = jnp.sum(gnt * n, axis=0, keepdims=True)
    sums_out[1:2, :] = jnp.sum(gnt, axis=0, keepdims=True)
    sums_out[2:3, :] = jnp.sum(gres, axis=0, keepdims=True)
    o0[...] = mm(gb, wo0[...], NT).astype(bf16)
    for k, o in enumerate((o1, o2, o3)):
        o[...] = mm(gb, wo[k], NT).astype(bf16)


def k_dw_out(z_ref, a0, a1, a2, a3, b0, b1, b2, b3, gb_a, gb_b, out):
    gb = jnp.concatenate([gb_a[...], gb_b[...]], axis=0)
    for r, (a, b) in enumerate(((a0, b0), (a1, b1), (a2, b2), (a3, b3))):
        out[r] = mm(jnp.concatenate([a[...], b[...]], axis=0), gb, TN).astype(bf16)


def k_attend_back(z_ref, q, k, v, p_a, p_b, ctx_a, ctx_b, e0, e1, e2, e3, f0, f1, f2, f3,
                  out, sums_out, gc, gs, cx):
    i = pl.program_id(0)
    z = z_ref[0]
    rows = e0.shape[0]
    total = q.shape[0]
    w = out.shape[1] // 3
    half = total // 2
    for h, es in enumerate(((e0, e1, e2, e3), (f0, f1, f2, f3))):
        for j, e in enumerate(es):
            at = h * half + jnp.bitwise_xor(z, j) * rows
            gc[pl.ds(pl.multiple_of(at, rows), rows), :] = e[...]
    cx[:half] = ctx_a[...]
    cx[half:] = ctx_b[...]
    low = low_lanes((total, 2 * HD))
    qp, kp, vp = q[...], k[...], v[...]
    gcv = gc[...]
    prod = gcv.astype(f32) * cx[...].astype(f32)
    gq, gk, gv = [], [], []
    for side in range(2):
        pick = low if side == 0 else ~low
        delta = jnp.sum(jnp.where(pick, prod, 0.0), axis=-1, keepdims=True)
        gm = jnp.where(pick, gcv, jnp.zeros_like(gcv))
        tile = 256
        for t in range(total // tile):
            at = slice(t * tile, (t + 1) * tile)
            gp = mm(gm[at], vp, NT)
            p = p_a if t * tile < half else p_b
            pt = p[side, t * tile % half:t * tile % half + tile, :].astype(f32)
            gs[at, :] = (pt * (gp - delta[at])).astype(bf16)
        gsv = gs[...]
        gq.append(mm(gsv, kp))
        gk.append(mm(qp, gsv, TN))
        gv.append(mm(gcv[:half], p_a[side], TN) + mm(gcv[half:], p_b[side], TN))
    gqv = (jnp.where(low, gq[0], gq[1]) * 0.125).astype(bf16)
    out[:, lane_ds(i * 2 * HD, 2 * HD)] = gqv
    top = lax.broadcasted_iota(jnp.int32, gk[0].shape, 0) < HD
    out[:, lane_ds(w + i * 2 * HD, 2 * HD)] = jnp.where(top, gk[0], gk[1]).T.astype(bf16)
    gvv = jnp.where(top, gv[0], gv[1]).T.astype(bf16)
    out[:, lane_ds(2 * w + i * 2 * HD, 2 * HD)] = gvv
    sums_out[...] = jnp.zeros_like(sums_out)
    sums_out[0:1, :] = jnp.sum(gqv.astype(f32), axis=0, keepdims=True)
    sums_out[1:2, :] = jnp.sum(gvv.astype(f32), axis=0, keepdims=True)


def k_norm_one(z_ref, g, wqkv, x, gains, gres_a, gres_b, sum_a, sum_b, o0, o1, o2, o3, mix, scr):
    i = pl.program_id(0)
    z = z_ref[0]
    w = o0.shape[1]
    gn = mm(g[...], wqkv[...], NT)
    m, c, r = norm_stats(x[...].astype(f32))
    n = c * r
    e = gn * gains[0:1, :]
    se = jnp.sum(e, axis=-1, keepdims=True)
    de = jnp.sum(e * n, axis=-1, keepdims=True)
    rows = gn.shape[0]
    lane = lax.broadcasted_iota(jnp.int32, (rows, 128), 1)
    cols = jnp.where(lane == 0, se, jnp.where(lane == 1, de, 0.0))
    scr[...] = r * e
    seg = gres_a.shape[0]
    per_half = pl.num_programs(0) // 2
    for h, gres in enumerate((gres_a, gres_b)):
        @pl.when(i == h * per_half + (z * seg) // rows)
        def _():
            scr[pl.ds(pl.multiple_of((z * seg) % rows, seg), seg), :] += gres[...]

    for r, o in enumerate((o0, o1, o2, o3)):
        o[...] = scr[:, lane_ds(jnp.bitwise_xor(z, r) * w, w)].astype(bf16)

    @pl.when(i == 0)
    def _():
        mix[2:4, :] = jnp.zeros((2, D), f32)
        mix[4:8, :] = sum_a[0:4, :] + sum_b[0:4, :]

    mix[0:2, lane_ds(i * rows, rows)] = cols.T[0:2, :]
    mix[2:3, :] += jnp.sum(gn * n, axis=0, keepdims=True)
    mix[3:4, :] += jnp.sum(gn, axis=0, keepdims=True)


def k_final(z_ref, t0, t1, t2, stats, nl, r, out):
    total = t0[...].astype(f32) + t1[...].astype(f32) + t2[...].astype(f32)
    cols = jnp.concatenate([stats[...]] * 16, 0).T * (1.0 / D)
    out[...] = (total - r[:, 0:1] * (cols[:, 0:1] + nl[...] * cols[:, 1:2])).astype(bf16)


def mask_bias(random_rows, length):
    heads = random_rows.shape[0]
    rows = jnp.arange(NB, dtype=jnp.int32)[:, None]
    cols = jnp.arange(NB, dtype=jnp.int32)[None, :]
    fixed = (
        (rows == 0) | (rows == NB - 1) | (cols == 0) | (cols == NB - 1)
        | (jnp.abs(rows - cols) <= 1)
    )
    chosen = jnp.any(random_rows[:, :, :, None] == cols[0][None, None, None, :], axis=2)
    allowed = jnp.transpose(fixed[None] | chosen, (1, 0, 2)).reshape(NB * heads, NB)
    valid = jnp.arange(LEN, dtype=jnp.int32) < length
    return jnp.where(jnp.repeat(allowed, BLOCK, axis=1) & valid[None, :], 0.0, -1e30).astype(f32)


def make_shards(dp, tp):
    def shards(inputs, lengths, random_blocks, attn_norm_gain, attn_norm_bias, query_weight,
               query_bias, key_weight, value_weight, value_bias, out_weight, out_bias,
               ffn_norm_gain, ffn_norm_bias, up_weight, up_bias, down_weight, down_bias, grad_out):
        tokens, w = inputs.shape
        ff = up_weight.shape[1]
        heads = w // HD
        half = tokens // 2
        quarter = tokens // tp
        tile = 256
        zi = lax.axis_index("tensor")
        z = zi.astype(jnp.int32).reshape(1)
        d_i = lax.axis_index("dp")

        seg = half // tp
        here_dp = dp_position(dp)
        part_rows = w // dp
        wo_part = lax.dynamic_slice_in_dim(out_weight, here_dp * part_rows, part_rows, 0)
        wo_in = jnp.stack([across(wo_part, r, tp) for r in range(1, tp)])
        far_in = across(inputs, 2, tp)
        near_in = across(inputs, 1, tp)
        small = jnp.concatenate(
            [attn_norm_gain, attn_norm_bias, out_bias, ffn_norm_gain, ffn_norm_bias, query_bias,
             value_bias, down_bias, jnp.zeros((8 * w,), bf16)]).reshape(16, w)
        packs = [small] + [across(small, r, tp) for r in range(1, tp)]
        last_in = across(after(far_in, near_in, packs), 1, tp)
        slots = [inputs, near_in, far_in, last_in]
        wo_pieces = dp_gather(wo_in, dp)
        wqkv = jnp.concatenate([query_weight, key_weight, value_weight], 1)
        bias = mask_bias(random_blocks[0], lengths[0])

        tw, td = rows_of((tile, w)), rows_of((tile, D))
        x_full, n_one, q, k, v, n_loc, r_one, gains = call(
            k_qkv, "qkv", (tokens // tile,),
            [tw] * 4 + [const((16, w))] * 4 + [const((D, 3 * w))],
            [td, td, tw, tw, tw, tw, rows_of((tile, 128)), const((16, D))],
            [sds((tokens, D), bf16), sds((tokens, D), bf16), sds((tokens, w), bf16),
             sds((tokens, w), bf16), sds((tokens, w), bf16), sds((tokens, w), f32),
             sds((tokens, 128), f32), sds((16, D), f32)],
        )(z, *slots, *packs, after(wqkv, bias))
        gos = lax.all_gather(after(grad_out, last_in), "tensor")

        nblk = tile // BLOCK
        att = []
        for h in range(2):
            steps = half // tile
            base = h * steps
            q_in = q if h == 0 else after(q, att[0][0])
            att.append(call(
                k_attend, "attend", (steps,),
                [pl.BlockSpec((tile, w), lambda i, z, base=base: (i + base, 0)),
                 const((tokens, w)), const((tokens, w)),
                 pl.BlockSpec((nblk * heads, LEN), lambda i, z, base=base: (i + base, 0))],
                [tw, pl.BlockSpec((heads, tile, LEN), lambda i, z: (0, i, 0))],
                [sds((half, w), bf16), sds((heads, half, LEN), bf16)],
                flops=2 * half * LEN * 128 * heads * 2, nbytes=8 << 20,
            )(z, q_in, k, v, bias))
        ctxs = [gather4(att[h][0], tp) for h in range(2)]

        (wo_rest,) = assemble((after(wo_pieces[0], att[1][0]), wo_pieces[1]), dp, bf16, axis=1)

        ffn = []
        carried = []
        for h in range(2):
            steps = half // tile
            base = h * steps
            here = lambda i, z, base=base: (i + base, 0)
            hw, hd, hf = (pl.BlockSpec((tile, n), here) for n in (w, D, ff))
            n_in = 18
            out = call(
                partial(k_ffn, base), "ffn", (steps,),
                [tw] * 4 + [pl.BlockSpec((tp, tile, w), lambda i, z, base=base: (0, i + base, 0)), hw,
                            hd, const((16, D)), const((w, D)), const((tp - 1, w, D)),
                                       const((D, ff)), const((1, ff)), const((ff, D))]
                + [pl.BlockSpec(memory_space=pl.ANY)] * len(carried),
                [hd, hd, hd, hf, hf, hw, hw, hw, hw] + [const((seg, D))] * 4 + [const((8, ff))],
                [sds((tokens, D), bf16), sds((tokens, D), f32), sds((tokens, D), bf16),
                 sds((tokens, ff), bf16), sds((tokens, ff), bf16), sds((tokens, w), f32)]
                + [sds((tokens, w), bf16)] * 3 + [sds((seg, D), bf16)] * 4 + [sds((8, ff), f32)],
                flops=2 * half * D * ff * 5, nbytes=24 << 20,
                aliases={14 + j: j for j in range(len(carried))},
            )(z, *ctxs[h], gos, grad_out, x_full, gains, out_weight, wo_rest, up_weight,
              up_bias.reshape(1, ff), down_weight, *carried)
            carried = out[:9]
            ffn.append(out)
        go_full, res_full, n_two, act, gup, d0, d1, d2, d3 = carried

        groups = stages(dp)
        dw_up = mm(n_two, gup, TN).astype(bf16)
        dw_down = mm(act, go_full, TN).astype(bf16)
        g_up, g_down = lax.psum((dw_up, dw_down), "dp")

        two = []
        for h in range(2):
            h0, h1, h2 = scatter4(ffn[h][9:13], tp)
            h0 = after(h0, dw_up, dw_down) if h == 0 else after(h0, two[0][1])
            at_z = pl.BlockSpec((seg, D), lambda i, z, h=h: (h * tp + z[0], 0))
            two.append(call(
                k_norm_two, "norm_two", (1,),
                [const((seg, D))] * 3 + [at_z, at_z, const((16, D)), const((w, D)),
                                         const((tp - 1, w, D))],
                [const((seg, D)), const((seg, D))] + [const((seg, w))] * 4 + [const((8, D))],
                [sds((seg, D), f32), sds((seg, D), bf16)] + [sds((seg, w), bf16)] * 4
                + [sds((8, D), f32)],
                flops=2 * seg * D * D, nbytes=10 << 20,
            )(z, h0, h1, h2, res_full, go_full, gains, out_weight, wo_rest))
        g_ctx = [[two[h][2]] + [across(two[h][2 + r], r, tp) for r in range(1, tp)]
                 for h in range(2)]
        seg_z = pl.BlockSpec((seg, w), lambda i, z: (z[0], 0))
        dw_out = call(
            k_dw_out, "dw_out", (1,), [seg_z] * 8 + [const((seg, D))] * 2, const((tp, w, D)),
            sds((tp, w, D), bf16), flops=2 * 2 * seg * D * D, nbytes=5 << 20,
        )(z, *ctxs[0], *ctxs[1], after(two[0][1], g_ctx[0]), two[1][1])

        pair = pl.BlockSpec((tokens, 2 * HD), lambda i, z: (0, i))
        pairh = pl.BlockSpec((half, 2 * HD), lambda i, z: (0, i))
        probs = pl.BlockSpec((2, half, LEN), lambda i, z: (i, 0, 0))
        out_part = dp_scatter(dw_out, dp, axis=1, groups=groups[:1])
        gqkv, sums_qkv = call(
            k_attend_back, "attend_back", (heads // 2,),
            [pair, pair, pair, probs, probs, pairh, pairh]
            + [pl.BlockSpec((seg, 2 * HD), lambda i, z: (0, i))] * 8,
            [const((tokens, 3 * w)), pl.BlockSpec((8, 2 * HD), lambda i, z: (0, i))],
            [sds((tokens, 3 * w), bf16), sds((8, w), f32)],
            scratch=[pltpu.VMEM((tokens, 2 * HD), bf16), pltpu.VMEM((tokens, LEN), bf16),
                     pltpu.VMEM((tokens, 2 * HD), bf16)],
        )(z, after(q, out_part), k, v, att[0][1], att[1][1], att[0][0], att[1][0], *g_ctx[0], *g_ctx[1])

        (d1, d2, d3) = after((d1, d2, d3), g_ctx)
        down_got3 = across(d3, 1, tp)
        down_got1 = across(d1, 1, tp)
        down_far = (after(d2, gqkv).astype(f32) + down_got3.astype(f32)).astype(bf16)
        down_got2 = across(down_far, 2, tp)
        outputs = (d0 + down_got1.astype(f32) + down_got2.astype(f32)).astype(bf16)
        out_part = dp_scatter(out_part, dp, axis=1, groups=groups[1:])
        g_in = after(gqkv, down_far, down_got1, out_part)
        *contrib, mix = call(
            k_norm_one, "norm_one", (tokens // tile,),
            [rows_of((tile, 3 * w)), const((D, 3 * w)), td, const((16, D)), const((seg, D)),
             const((seg, D)), const((8, D)), const((8, D))],
            [tw] * 4 + [const((8, D))], [sds((tokens, w), bf16)] * 4 + [sds((8, D), f32)],
            scratch=[pltpu.VMEM((tile, D), f32)],
        )(z, g_in, wqkv, x_full, gains, two[0][0], two[1][0], two[0][6], two[1][6])

        got3 = across(contrib[3], 1, tp)
        got1 = across(contrib[1], 1, tp)
        far = (contrib[2].astype(f32) + got3.astype(f32)).astype(bf16)
        totals = [contrib[0], got1, across(far, 2, tp)]
        mix = sum4(mix, tp)

        out_got = [across(out_part[r], r, tp) for r in range(1, tp)]
        own = out_part[0].astype(f32)
        for got in out_got:
            own = own + got.astype(f32)
        own = own.astype(bf16)
        dw_qkv = mm(n_one, after(gqkv, contrib), TN).astype(bf16)
        qkv_part = dp_scatter(dw_qkv, dp, groups=groups[:1])
        qkv_part = dp_scatter(after(qkv_part, mix, far, got1, own), dp, groups=groups[1:])
        out_one, out_two = dp_gather(own, dp)
        (g_out_w,) = assemble((out_one, out_two), dp, f32)
        qkv_one = dp_gather_near(after(qkv_part, out_one), dp)
        qkv_two = swap(after(qkv_one, totals, g_out_w, g_up), 1, dp)
        g_up, g_down = g_up.astype(f32), g_down.astype(f32)
        g_q, g_k, g_v = assemble((qkv_one, qkv_two), dp, f32, outs=3)

        grad_inputs = call(
            k_final, "final", (tokens // tile,),
            [tw] * 3 + [pl.BlockSpec((8, tile), lambda i, z: (0, i)), tw, rows_of((tile, 128))],
            tw, sds((tokens, w), bf16),
        )(z, *totals, mix, n_loc, r_one)

        mine = lax.dynamic_slice(mix, (2, zi * w), (5, w))
        up_sum = ffn[0][-1] + ffn[1][-1]
        vec = jnp.concatenate([mine, sums_qkv[0:2], up_sum[1:2, :w], up_sum[0:1].reshape(-1, w)], 0)
        vec = dp_sum_small(vec, dp).reshape(-1)
        pieces = [vec[j * w:(j + 1) * w] for j in range(8)]
        g_up_b = vec[8 * w:]
        return (outputs, grad_inputs, pieces[0], pieces[1], g_q, pieces[5], g_k, g_v, pieces[6],
                g_out_w, pieces[4], pieces[2], pieces[3], g_up, g_up_b, g_down, pieces[7])

    return shards


def solution(mesh):
    return jax.shard_map(
        make_shards(mesh.shape["dp"], mesh.shape["tensor"]),
        mesh=mesh,
        in_specs=(
            P("dp", "tensor"), P("dp"), P("dp", "tensor", None, None), P("tensor"), P("tensor"),
            P(None, "tensor"), P("tensor"), P(None, "tensor"), P(None, "tensor"), P("tensor"),
            P("tensor", None), P("tensor"), P("tensor"), P("tensor"), P(None, "tensor"),
            P("tensor"), P("tensor", None), P("tensor"), P("dp", "tensor"),
        ),
        out_specs=(
            P("dp", "tensor"), P("dp", "tensor"), P("tensor"), P("tensor"), P(None, "tensor"),
            P("tensor"), P(None, "tensor"), P(None, "tensor"), P("tensor"), P("tensor", None),
            P("tensor"), P("tensor"), P("tensor"), P(None, "tensor"), P("tensor"),
            P("tensor", None), P("tensor"),
        ),
        check_vma=False,
    )
```

```python
from functools import partial

import jax
import jax.numpy as jnp
from jax import lax
from jax.experimental import pallas as pl
from jax.experimental.pallas import tpu as pltpu
from jax.sharding import PartitionSpec as P

D = 1024
HD = 64
BLOCK = 64
LEN = 1024
NB = 16
EPS = 1e-05
VMEM_LIMIT = {"qkv": 60, "attend": 24, "ffn": 60, "norm_two": 60, "attend_back": 60, "norm_one": 24, "final": 16,
              "widen": 60, "assemble": 24, "dw_out": 20}
f32 = jnp.float32
bf16 = jnp.bfloat16
NT = (((1,), (1,)), ((), ()))
NN = (((1,), (0,)), ((), ()))
TN = (((0,), (0,)), ((), ()))


def mm(left, right, dims=NN):
    return lax.dot_general(left, right, dims, preferred_element_type=f32)


def call(kernel, name, grid, in_specs, out_specs, out_shape, scratch=(), flops=0, nbytes=0,
         aliases=None):
    return pl.pallas_call(
        kernel,
        out_shape=out_shape,
        grid_spec=pltpu.PrefetchScalarGridSpec(
            num_scalar_prefetch=1,
            grid=grid,
            in_specs=in_specs,
            out_specs=out_specs,
            scratch_shapes=list(scratch),
        ),
        compiler_params=pltpu.CompilerParams(
            dimension_semantics=("arbitrary",) * len(grid), vmem_limit_bytes=VMEM_LIMIT[name] << 20
        ),
        cost_estimate=pl.CostEstimate(flops=0, bytes_accessed=0, transcendentals=0),
        input_output_aliases=aliases or {},
        name=name,
    )


def sds(shape, dtype):
    return jax.ShapeDtypeStruct(shape, dtype)


def hbm(shape, dtype):
    return pltpu.HBM(shape, dtype)


def const(shape):
    return pl.BlockSpec(shape, lambda i, z: (0,) * len(shape))


def rows_of(shape):
    return pl.BlockSpec(shape, lambda i, z: (i,) + (0,) * (len(shape) - 1))


def lane_ds(start, size):
    return pl.ds(pl.multiple_of(start, 128), size)


def after(value, *others):
    return lax.optimization_barrier((value, others))[0]


def across(value, mask, size):
    return lax.ppermute(value, "tensor", [(i, i ^ mask) for i in range(size)])


def swap(value, mask, size):
    return lax.ppermute(value, "dp", [(i, i ^ mask) for i in range(size)])


def gather4(value, size):
    far = across(value, 2, size)
    near = across(value, 1, size)
    return [value, near, far, across(far, 1, size)]


def scatter4(slots, size):
    got3 = across(slots[3], 1, size)
    got1 = across(slots[1], 1, size)
    far = (slots[2].astype(f32) + got3.astype(f32)).astype(slots[2].dtype)
    return slots[0], got1, across(far, 2, size)


def sum4(value, size):
    value = value + across(value, 1, size)
    return value + across(value, 2, size)


def stages(size):
    bits = list(range(size.bit_length() - 1))
    return [bits[:1]] + [bits[j:j + 2] for j in range(1, len(bits), 2)]


def digit_of(index, group):
    digit = 0
    for j, bit in enumerate(group):
        digit = digit | (((index >> bit) & 1) << j)
    return digit


def mask_of(k, group):
    return sum(((k >> j) & 1) << bit for j, bit in enumerate(group))


def dp_position(size):
    index = lax.axis_index("dp")
    place = 0
    for group in stages(size):
        place = (place << len(group)) | digit_of(index, group)
    return place.astype(jnp.int32)


def dp_scatter(value, size, axis=0, groups=None):
    index = lax.axis_index("dp")
    for group in stages(size) if groups is None else groups:
        n = 1 << len(group)
        mine = digit_of(index, group)
        rows = value.shape[axis] // n
        take = lambda at: lax.dynamic_slice_in_dim(value, at * rows, rows, axis)
        got = [swap(take(mine ^ k), mask_of(k, group), size) for k in range(1, n)]
        total = take(mine).astype(f32)
        for g in got:
            total = total + g.astype(f32)
        value = total.astype(value.dtype)
    return value


def dp_gather_near(value, size):
    value = value[None]
    for group in stages(size)[1:][::-1]:
        n = 1 << len(group)
        value = jnp.stack([value] + [swap(value, mask_of(k, group), size) for k in range(1, n)])
        value = value.reshape((-1,) + value.shape[2:])
    return value


def dp_gather(value, size):
    one = dp_gather_near(value, size)
    return one, swap(one, 1, size)


def dp_sum_small(value, size):
    for bit in range(size.bit_length() - 1):
        value = value + swap(value, 1 << bit, size)
    return value


def k_assemble(axis, p_ref, one, two, *outs):
    n, rows = one.shape[0], one.shape[1 + axis]
    w = outs[0].shape[-1]
    for flip, value in ((0, one), (1, two)):
        for k in range(n):
            at = pl.ds(pl.multiple_of(jnp.bitwise_xor(p_ref[0], flip * n + k) * rows, rows), rows)
            block = value[k]
            for j, out in enumerate(outs):
                out[(slice(None),) * axis + (at,)] = block[..., j * w:(j + 1) * w].astype(out.dtype)


def assemble(pieces, size, dtype, outs=1, axis=0):
    one, two = pieces
    n = 2 * one.shape[0]
    block = list(one.shape[1:])
    if block[axis] % 16:
        order = jnp.bitwise_xor(jnp.arange(n, dtype=jnp.int32), dp_position(size))
        ordered = jnp.moveaxis(jnp.concatenate([one, two], 0)[order], 0, axis)
        shape = block[:axis] + [n * block[axis]] + block[axis + 1:]
        return jnp.split(ordered.reshape(shape).astype(dtype), outs, axis=-1)
    whole = list(block)
    whole[-1] //= outs
    whole[axis] *= n
    return call(
        partial(k_assemble, axis), "assemble", (1,), [const(one.shape)] * 2,
        [const(tuple(whole))] * outs, [sds(tuple(whole), dtype)] * outs, nbytes=12 * one.size,
    )(dp_position(size).reshape(1), one, two)


def norm_stats(x):
    m = jnp.mean(x, axis=-1, keepdims=True)
    c = x - m
    r = lax.rsqrt(jnp.mean(c * c, axis=-1, keepdims=True) + EPS)
    return m, c, r


def k_qkv(z_ref, x0, x1, x2, x3, s0, s1, s2, s3, wqkv,
          x_out, n_out, q_out, k_out, v_out, nl_out, r_out, g_out):
    z = z_ref[0]
    w = x0.shape[1]
    for r, (xb, s) in enumerate(((x0, s0), (x1, s1), (x2, s2), (x3, s3))):
        at = lane_ds(jnp.bitwise_xor(z, r) * w, w)
        x_out[:, at] = xb[...]
        g_out[:, at] = s[0:16, :].astype(f32)
    m, c, r = norm_stats(x_out[...].astype(f32))
    n = (c * r * g_out[0:1, :] + g_out[1:2, :]).astype(bf16)
    n_out[...] = n
    nl_out[...] = (x0[...].astype(f32) - m) * r
    r_out[...] = jnp.broadcast_to(r, r_out.shape)
    small = s0[0:16, :].astype(f32)
    full = mm(n, wqkv[...])
    q_out[...] = ((full[:, :w] + small[5:6, :]).astype(bf16) * 0.125).astype(bf16)
    k_out[...] = full[:, w:2 * w].astype(bf16)
    v_out[...] = (full[:, 2 * w:] + small[6:7, :]).astype(bf16)


def low_lanes(shape):
    return lax.broadcasted_iota(jnp.int32, shape, len(shape) - 1) < HD


def k_attend(z_ref, q, k, v, bias, ctx_out, p_out):
    rows = q.shape[0]
    nblk = rows // BLOCK
    low = low_lanes((rows, 2 * HD))
    heads = q.shape[1] // HD
    for pair in range(heads // 2):
        lanes = slice(pair * 2 * HD, (pair + 1) * 2 * HD)
        qp = q[:, lanes]
        kp = k[:, lanes]
        vp = v[:, lanes]
        parts = []
        for side in range(2):
            h = pair * 2 + side
            qm = jnp.where(low if side == 0 else ~low, qp, jnp.zeros_like(qp))
            s = mm(qm, kp, NT)
            pieces = []
            for b in range(nblk):
                sb = s[b * BLOCK:(b + 1) * BLOCK] + bias[b * heads + h:b * heads + h + 1, :]
                top = jnp.max(sb, axis=-1, keepdims=True)
                e = jnp.exp(sb - top)
                total = jnp.sum(e, axis=-1, keepdims=True)
                pieces.append((e * (1.0 / total)).astype(bf16))
            p = jnp.concatenate(pieces, 0)
            p_out[h] = p
            parts.append(mm(p, vp))
        ctx_out[:, lanes] = jnp.where(low, parts[0], parts[1]).astype(bf16)


def k_ffn(base, z_ref, c0, c1, c2, c3, gs, g_own, x, gains, wo0, wo, wu, ub, wd, *rest):
    (go_out, res_out, n_out, act_out, gup_out, d0, d1, d2, d3,
     h0, h1, h2, h3, sums_out) = rest[-14:]
    i = pl.program_id(0)
    z = z_ref[0]
    w = c0.shape[1]
    attn = mm(c0[...], wo0[...])
    for r, c in enumerate((c1, c2, c3)):
        attn = attn + mm(c[...], wo[r])
    for j in range(gs.shape[0]):
        go_out[:, j * w:(j + 1) * w] = gs[j]
    resid = x[...].astype(f32) + attn + gains[2:3, :]
    res_out[...] = resid
    m, c, r = norm_stats(resid)
    n = (c * r * gains[3:4, :] + gains[4:5, :]).astype(bf16)
    n_out[...] = n
    u = mm(n, wu[...]) + ub[...].astype(f32)
    uu = u * u
    t = jnp.tanh(0.7978845608028654 * u * (1.0 + 0.044715 * uu))
    half = 0.5 * (1.0 + t)
    act = (u * half).astype(bf16)
    slope = half + 0.5 * u * (1.0 - t * t) * (0.7978845608028654 * (1.0 + 0.134145 * uu))
    act_out[...] = act
    gup = (mm(go_out[...], wd[...], NT) * slope).astype(bf16)
    gup_out[...] = gup
    gnt = mm(gup, wu[...], NT).astype(bf16)
    seg = h0.shape[0]
    per = gnt.shape[0] // seg
    for s in range(per):
        for r, h in enumerate((h0, h1, h2, h3)):
            @pl.when(jnp.bitwise_xor(i * per + s, z) == r)
            def _():
                h[...] = gnt[s * seg:(s + 1) * seg]

    own = lane_ds(z * w, w)
    d0[...] = res_out[:, own] + mm(act, wd[:, own]) + gains[7:8, own]
    for r, d in ((1, d1), (2, d2), (3, d3)):
        d[...] = mm(act, wd[:, lane_ds(jnp.bitwise_xor(z, r) * w, w)]).astype(bf16)

    @pl.when(i == 0)
    def _():
        sums_out[...] = jnp.zeros_like(sums_out)

    sums_out[0:1, :] += jnp.sum(gup.astype(f32), axis=0, keepdims=True)
    sums_out[1:2, 0:w] += jnp.sum(g_own[...].astype(f32), axis=0, keepdims=True)


def k_norm_two(z_ref, h0, h1, h2, resid, go, gains, wo0, wo, gr_out, gb_out, o0, o1, o2, o3, sums_out):
    gnt = h0[...].astype(f32) + h1[...].astype(f32) + h2[...].astype(f32)
    m, c, r = norm_stats(resid[...])
    n = c * r
    e = gnt * gains[3:4, :]
    me = jnp.mean(e, axis=-1, keepdims=True)
    mn = jnp.mean(e * n, axis=-1, keepdims=True)
    gres = go[...].astype(f32) + r * (e - me - n * mn)
    gr_out[...] = gres
    gb = gres.astype(bf16)
    gb_out[...] = gb
    sums_out[...] = jnp.zeros_like(sums_out)
    sums_out[0:1, :] = jnp.sum(gnt * n, axis=0, keepdims=True)
    sums_out[1:2, :] = jnp.sum(gnt, axis=0, keepdims=True)
    sums_out[2:3, :] = jnp.sum(gres, axis=0, keepdims=True)
    o0[...] = mm(gb, wo0[...], NT).astype(bf16)
    for k, o in enumerate((o1, o2, o3)):
        o[...] = mm(gb, wo[k], NT).astype(bf16)


def k_dw_out(z_ref, a0, a1, a2, a3, b0, b1, b2, b3, gb_a, gb_b, out):
    gb = jnp.concatenate([gb_a[...], gb_b[...]], axis=0)
    for r, (a, b) in enumerate(((a0, b0), (a1, b1), (a2, b2), (a3, b3))):
        out[r] = mm(jnp.concatenate([a[...], b[...]], axis=0), gb, TN).astype(bf16)


def k_attend_back(z_ref, q, k, v, p_a, p_b, ctx_a, ctx_b, e0, e1, e2, e3, f0, f1, f2, f3,
                  out, sums_out, gc, gs, cx):
    i = pl.program_id(0)
    z = z_ref[0]
    rows = e0.shape[0]
    total = q.shape[0]
    w = out.shape[1] // 3
    half = total // 2
    for h, es in enumerate(((e0, e1, e2, e3), (f0, f1, f2, f3))):
        for j, e in enumerate(es):
            at = h * half + jnp.bitwise_xor(z, j) * rows
            gc[pl.ds(pl.multiple_of(at, rows), rows), :] = e[...]
    cx[:half] = ctx_a[...]
    cx[half:] = ctx_b[...]
    low = low_lanes((total, 2 * HD))
    qp, kp, vp = q[...], k[...], v[...]
    gcv = gc[...]
    prod = gcv.astype(f32) * cx[...].astype(f32)
    gq, gk, gv = [], [], []
    for side in range(2):
        pick = low if side == 0 else ~low
        delta = jnp.sum(jnp.where(pick, prod, 0.0), axis=-1, keepdims=True)
        gm = jnp.where(pick, gcv, jnp.zeros_like(gcv))
        tile = 256
        for t in range(total // tile):
            at = slice(t * tile, (t + 1) * tile)
            gp = mm(gm[at], vp, NT)
            p = p_a if t * tile < half else p_b
            pt = p[side, t * tile % half:t * tile % half + tile, :].astype(f32)
            gs[at, :] = (pt * (gp - delta[at])).astype(bf16)
        gsv = gs[...]
        gq.append(mm(gsv, kp))
        gk.append(mm(qp, gsv, TN))
        gv.append(mm(gcv[:half], p_a[side], TN) + mm(gcv[half:], p_b[side], TN))
    gqv = (jnp.where(low, gq[0], gq[1]) * 0.125).astype(bf16)
    out[:, lane_ds(i * 2 * HD, 2 * HD)] = gqv
    top = lax.broadcasted_iota(jnp.int32, gk[0].shape, 0) < HD
    out[:, lane_ds(w + i * 2 * HD, 2 * HD)] = jnp.where(top, gk[0], gk[1]).T.astype(bf16)
    gvv = jnp.where(top, gv[0], gv[1]).T.astype(bf16)
    out[:, lane_ds(2 * w + i * 2 * HD, 2 * HD)] = gvv
    sums_out[...] = jnp.zeros_like(sums_out)
    sums_out[0:1, :] = jnp.sum(gqv.astype(f32), axis=0, keepdims=True)
    sums_out[1:2, :] = jnp.sum(gvv.astype(f32), axis=0, keepdims=True)


def k_norm_one(z_ref, g, wqkv, x, gains, gres_a, gres_b, sum_a, sum_b, o0, o1, o2, o3, mix, scr):
    i = pl.program_id(0)
    z = z_ref[0]
    w = o0.shape[1]
    gn = mm(g[...], wqkv[...], NT)
    m, c, r = norm_stats(x[...].astype(f32))
    n = c * r
    e = gn * gains[0:1, :]
    se = jnp.sum(e, axis=-1, keepdims=True)
    de = jnp.sum(e * n, axis=-1, keepdims=True)
    rows = gn.shape[0]
    lane = lax.broadcasted_iota(jnp.int32, (rows, 128), 1)
    cols = jnp.where(lane == 0, se, jnp.where(lane == 1, de, 0.0))
    scr[...] = r * e
    seg = gres_a.shape[0]
    per_half = pl.num_programs(0) // 2
    for h, gres in enumerate((gres_a, gres_b)):
        @pl.when(i == h * per_half + (z * seg) // rows)
        def _():
            scr[pl.ds(pl.multiple_of((z * seg) % rows, seg), seg), :] += gres[...]

    for r, o in enumerate((o0, o1, o2, o3)):
        o[...] = scr[:, lane_ds(jnp.bitwise_xor(z, r) * w, w)].astype(bf16)

    @pl.when(i == 0)
    def _():
        mix[2:4, :] = jnp.zeros((2, D), f32)
        mix[4:8, :] = sum_a[0:4, :] + sum_b[0:4, :]

    mix[0:2, lane_ds(i * rows, rows)] = cols.T[0:2, :]
    mix[2:3, :] += jnp.sum(gn * n, axis=0, keepdims=True)
    mix[3:4, :] += jnp.sum(gn, axis=0, keepdims=True)


def k_widen(z_ref, up, down, vec, up_out, down_out):
    up_out[...] = up[...].astype(f32)
    down_out[...] = down[...].astype(f32)


def k_final(z_ref, t0, t1, t2, stats, nl, r, out):
    total = t0[...].astype(f32) + t1[...].astype(f32) + t2[...].astype(f32)
    cols = jnp.concatenate([stats[...]] * 16, 0).T * (1.0 / D)
    out[...] = (total - r[:, 0:1] * (cols[:, 0:1] + nl[...] * cols[:, 1:2])).astype(bf16)


def mask_bias(random_rows, length):
    heads = random_rows.shape[0]
    rows = jnp.arange(NB, dtype=jnp.int32)[:, None]
    cols = jnp.arange(NB, dtype=jnp.int32)[None, :]
    fixed = (
        (rows == 0) | (rows == NB - 1) | (cols == 0) | (cols == NB - 1)
        | (jnp.abs(rows - cols) <= 1)
    )
    chosen = jnp.any(random_rows[:, :, :, None] == cols[0][None, None, None, :], axis=2)
    allowed = jnp.transpose(fixed[None] | chosen, (1, 0, 2)).reshape(NB * heads, NB)
    valid = jnp.arange(LEN, dtype=jnp.int32) < length
    return jnp.where(jnp.repeat(allowed, BLOCK, axis=1) & valid[None, :], 0.0, -1e30).astype(f32)


def make_shards(dp, tp):
    def shards(inputs, lengths, random_blocks, attn_norm_gain, attn_norm_bias, query_weight,
               query_bias, key_weight, value_weight, value_bias, out_weight, out_bias,
               ffn_norm_gain, ffn_norm_bias, up_weight, up_bias, down_weight, down_bias, grad_out):
        tokens, w = inputs.shape
        ff = up_weight.shape[1]
        heads = w // HD
        half = tokens // 2
        quarter = tokens // tp
        tile = 256
        zi = lax.axis_index("tensor")
        z = zi.astype(jnp.int32).reshape(1)
        d_i = lax.axis_index("dp")

        seg = half // tp
        here_dp = dp_position(dp)
        part_rows = w // dp
        wo_part = lax.dynamic_slice_in_dim(out_weight, here_dp * part_rows, part_rows, 0)
        wo_in = jnp.stack([across(wo_part, r, tp) for r in range(1, tp)])
        far_in = across(inputs, 2, tp)
        near_in = across(inputs, 1, tp)
        small = jnp.concatenate(
            [attn_norm_gain, attn_norm_bias, out_bias, ffn_norm_gain, ffn_norm_bias, query_bias,
             value_bias, down_bias, jnp.zeros((8 * w,), bf16)]).reshape(16, w)
        packs = [small] + [across(small, r, tp) for r in range(1, tp)]
        last_in = across(after(far_in, near_in, packs), 1, tp)
        slots = [inputs, near_in, far_in, last_in]
        wo_pieces = dp_gather(wo_in, dp)
        wqkv = jnp.concatenate([query_weight, key_weight, value_weight], 1)
        bias = mask_bias(random_blocks[0], lengths[0])

        tw, td = rows_of((tile, w)), rows_of((tile, D))
        x_full, n_one, q, k, v, n_loc, r_one, gains = call(
            k_qkv, "qkv", (tokens // tile,),
            [tw] * 4 + [const((16, w))] * 4 + [const((D, 3 * w))],
            [td, td, tw, tw, tw, tw, rows_of((tile, 128)), const((16, D))],
            [hbm((tokens, D), bf16), hbm((tokens, D), bf16), sds((tokens, w), bf16),
             sds((tokens, w), bf16), sds((tokens, w), bf16), hbm((tokens, w), f32),
             hbm((tokens, 128), f32), sds((16, D), f32)],
        )(z, *slots, *packs, after(wqkv, bias))
        gos = lax.all_gather(after(grad_out, last_in), "tensor")

        nblk = tile // BLOCK
        att = []
        for h in range(2):
            steps = half // tile
            base = h * steps
            q_in = q if h == 0 else after(q, att[0][0])
            att.append(call(
                k_attend, "attend", (steps,),
                [pl.BlockSpec((tile, w), lambda i, z, base=base: (i + base, 0)),
                 const((tokens, w)), const((tokens, w)),
                 pl.BlockSpec((nblk * heads, LEN), lambda i, z, base=base: (i + base, 0))],
                [tw, pl.BlockSpec((heads, tile, LEN), lambda i, z: (0, i, 0))],
                [sds((half, w), bf16), hbm((heads, half, LEN), bf16)],
                flops=2 * half * LEN * 128 * heads * 2, nbytes=8 << 20,
            )(z, q_in, k, v, bias))
        ctxs = [gather4(att[h][0], tp) for h in range(2)]

        (wo_rest,) = assemble((after(wo_pieces[0], att[1][0]), wo_pieces[1]), dp, bf16, axis=1)

        ffn = []
        carried = []
        for h in range(2):
            steps = half // tile
            base = h * steps
            here = lambda i, z, base=base: (i + base, 0)
            hw, hd, hf = (pl.BlockSpec((tile, n), here) for n in (w, D, ff))
            n_in = 18
            out = call(
                partial(k_ffn, base), "ffn", (steps,),
                [tw] * 4 + [pl.BlockSpec((tp, tile, w), lambda i, z, base=base: (0, i + base, 0)), hw,
                            hd, const((16, D)), const((w, D)), const((tp - 1, w, D)),
                                       const((D, ff)), const((1, ff)), const((ff, D))]
                + [pl.BlockSpec(memory_space=pl.ANY)] * len(carried),
                [hd, hd, hd, hf, hf, hw, hw, hw, hw] + [const((seg, D))] * 4 + [const((8, ff))],
                [hbm((tokens, D), bf16), hbm((tokens, D), f32), hbm((tokens, D), bf16),
                 hbm((tokens, ff), bf16), hbm((tokens, ff), bf16), sds((tokens, w), f32)]
                + [sds((tokens, w), bf16)] * 3 + [sds((seg, D), bf16)] * 4 + [sds((8, ff), f32)],
                flops=2 * half * D * ff * 5, nbytes=24 << 20,
                aliases={14 + j: j for j in range(len(carried))},
            )(z, *ctxs[h], gos, grad_out, x_full, gains, out_weight, wo_rest, up_weight,
              up_bias.reshape(1, ff), down_weight, *carried)
            carried = out[:9]
            ffn.append(out)
        go_full, res_full, n_two, act, gup, d0, d1, d2, d3 = carried

        groups = stages(dp)
        dw_up = mm(n_two, gup, TN).astype(bf16)
        dw_down = mm(act, go_full, TN).astype(bf16)
        g_up, g_down = lax.psum((dw_up, dw_down), "dp")

        two = []
        for h in range(2):
            h0, h1, h2 = scatter4(ffn[h][9:13], tp)
            h0 = after(h0, dw_up, dw_down) if h == 0 else after(h0, two[0][1])
            at_z = pl.BlockSpec((seg, D), lambda i, z, h=h: (h * tp + z[0], 0))
            two.append(call(
                k_norm_two, "norm_two", (1,),
                [const((seg, D))] * 3 + [at_z, at_z, const((16, D)), const((w, D)),
                                         const((tp - 1, w, D))],
                [const((seg, D)), const((seg, D))] + [const((seg, w))] * 4 + [const((8, D))],
                [sds((seg, D), f32), sds((seg, D), bf16)] + [sds((seg, w), bf16)] * 4
                + [sds((8, D), f32)],
                flops=2 * seg * D * D, nbytes=10 << 20,
            )(z, h0, h1, h2, res_full, go_full, gains, out_weight, wo_rest))
        g_ctx = [[two[h][2]] + [across(two[h][2 + r], r, tp) for r in range(1, tp)]
                 for h in range(2)]
        seg_z = pl.BlockSpec((seg, w), lambda i, z: (z[0], 0))
        dw_out = call(
            k_dw_out, "dw_out", (1,), [seg_z] * 8 + [const((seg, D))] * 2, const((tp, w, D)),
            sds((tp, w, D), bf16), flops=2 * 2 * seg * D * D, nbytes=5 << 20,
        )(z, *ctxs[0], *ctxs[1], after(two[0][1], g_ctx[0]), two[1][1])

        pair = pl.BlockSpec((tokens, 2 * HD), lambda i, z: (0, i))
        pairh = pl.BlockSpec((half, 2 * HD), lambda i, z: (0, i))
        probs = pl.BlockSpec((2, half, LEN), lambda i, z: (i, 0, 0))
        out_part = dp_scatter(dw_out, dp, axis=1, groups=groups[:1])
        gqkv, sums_qkv = call(
            k_attend_back, "attend_back", (heads // 2,),
            [pair, pair, pair, probs, probs, pairh, pairh]
            + [pl.BlockSpec((seg, 2 * HD), lambda i, z: (0, i))] * 8,
            [const((tokens, 3 * w)), pl.BlockSpec((8, 2 * HD), lambda i, z: (0, i))],
            [sds((tokens, 3 * w), bf16), sds((8, w), f32)],
            scratch=[pltpu.VMEM((tokens, 2 * HD), bf16), pltpu.VMEM((tokens, LEN), bf16),
                     pltpu.VMEM((tokens, 2 * HD), bf16)],
        )(z, after(q, out_part), k, v, att[0][1], att[1][1], att[0][0], att[1][0], *g_ctx[0], *g_ctx[1])

        (d1, d2, d3) = after((d1, d2, d3), g_ctx)
        down_got3 = across(d3, 1, tp)
        down_got1 = across(d1, 1, tp)
        down_far = (after(d2, gqkv).astype(f32) + down_got3.astype(f32)).astype(bf16)
        down_got2 = across(down_far, 2, tp)
        outputs = (d0 + down_got1.astype(f32) + down_got2.astype(f32)).astype(bf16)
        out_part = dp_scatter(out_part, dp, axis=1, groups=groups[1:])
        g_in = after(gqkv, down_far, down_got1, out_part)
        *contrib, mix = call(
            k_norm_one, "norm_one", (tokens // tile,),
            [rows_of((tile, 3 * w)), const((D, 3 * w)), td, const((16, D)), const((seg, D)),
             const((seg, D)), const((8, D)), const((8, D))],
            [tw] * 4 + [const((8, D))], [sds((tokens, w), bf16)] * 4 + [sds((8, D), f32)],
            scratch=[pltpu.VMEM((tile, D), f32)],
        )(z, g_in, wqkv, x_full, gains, two[0][0], two[1][0], two[0][6], two[1][6])

        got3 = across(contrib[3], 1, tp)
        got1 = across(contrib[1], 1, tp)
        far = (after(contrib[2], down_got2).astype(f32) + got3.astype(f32)).astype(bf16)
        totals = [contrib[0], got1, across(far, 2, tp)]
        mix = sum4(mix, tp)

        out_got = [across(out_part[r], r, tp) for r in range(1, tp)]
        own = out_part[0].astype(f32)
        for got in out_got:
            own = own + got.astype(f32)
        own = own.astype(bf16)
        dw_qkv = mm(n_one, after(gqkv, contrib), TN).astype(bf16)
        qkv_part = dp_scatter(dw_qkv, dp, groups=groups[:1])
        qkv_part = dp_scatter(after(qkv_part, mix, far, got1, own), dp, groups=groups[1:])
        out_one, out_two = dp_gather(own, dp)
        (g_out_w,) = assemble((out_one, out_two), dp, f32)
        mine = lax.dynamic_slice(mix, (2, zi * w), (5, w))
        up_sum = ffn[0][-1] + ffn[1][-1]
        vec = jnp.concatenate([mine, sums_qkv[0:2], up_sum[1:2, :w], up_sum[0:1].reshape(-1, w)], 0)
        vec = dp_sum_small(vec, dp)
        qkv_part = after(qkv_part, g_up, totals, vec)
        blocks = rows_of((tile, D))
        g_up, g_down = call(
            k_widen, "widen", (D // tile,), [blocks, blocks, pl.BlockSpec(memory_space=pl.ANY)], [blocks, blocks], [sds((D, ff), f32), sds((ff, D), f32)],
        )(z, g_up, g_down, vec)
        vec = vec.reshape(-1)
        qkv_one = dp_gather_near(after(qkv_part, out_one), dp)
        qkv_two = swap(after(qkv_one, totals, g_out_w, g_up), 1, dp)
        g_q, g_k, g_v = assemble((qkv_one, qkv_two), dp, f32, outs=3)

        grad_inputs = call(
            k_final, "final", (tokens // tile,),
            [tw] * 3 + [pl.BlockSpec((8, tile), lambda i, z: (0, i)), tw, rows_of((tile, 128))],
            tw, sds((tokens, w), bf16),
        )(z, *totals, mix, n_loc, r_one)

        pieces = [vec[j * w:(j + 1) * w] for j in range(8)]
        g_up_b = vec[8 * w:]
        return (outputs, grad_inputs, pieces[0], pieces[1], g_q, pieces[5], g_k, g_v, pieces[6],
                g_out_w, pieces[4], pieces[2], pieces[3], g_up, g_up_b, g_down, pieces[7])

    return shards


def solution(mesh):
    return jax.shard_map(
        make_shards(mesh.shape["dp"], mesh.shape["tensor"]),
        mesh=mesh,
        in_specs=(
            P("dp", "tensor"), P("dp"), P("dp", "tensor", None, None), P("tensor"), P("tensor"),
            P(None, "tensor"), P("tensor"), P(None, "tensor"), P(None, "tensor"), P("tensor"),
            P("tensor", None), P("tensor"), P("tensor"), P("tensor"), P(None, "tensor"),
            P("tensor"), P("tensor", None), P("tensor"), P("dp", "tensor"),
        ),
        out_specs=(
            P("dp", "tensor"), P("dp", "tensor"), P("tensor"), P("tensor"), P(None, "tensor"),
            P("tensor"), P(None, "tensor"), P(None, "tensor"), P("tensor"), P("tensor", None),
            P("tensor"), P("tensor"), P("tensor"), P(None, "tensor"), P("tensor"),
            P("tensor", None), P("tensor"),
        ),
        check_vma=False,
    )
```

```python
from functools import partial

import jax
import jax.numpy as jnp
from jax import lax
from jax.experimental import pallas as pl
from jax.experimental.pallas import tpu as pltpu
from jax.sharding import PartitionSpec as P

D = 1024
HD = 64
BLOCK = 64
LEN = 1024
NB = 16
EPS = 1e-05
VMEM_LIMIT = {"qkv": 60, "attend": 24, "ffn": 60, "norm_two": 60, "attend_back": 60, "norm_one": 24, "final": 16,
              "widen": 60, "assemble": 24, "dw_out": 20}
f32 = jnp.float32
bf16 = jnp.bfloat16
NT = (((1,), (1,)), ((), ()))
NN = (((1,), (0,)), ((), ()))
TN = (((0,), (0,)), ((), ()))


def mm(left, right, dims=NN):
    return lax.dot_general(left, right, dims, preferred_element_type=f32)


def call(kernel, name, grid, in_specs, out_specs, out_shape, scratch=(), flops=0, nbytes=0,
         aliases=None):
    return pl.pallas_call(
        kernel,
        out_shape=out_shape,
        grid_spec=pltpu.PrefetchScalarGridSpec(
            num_scalar_prefetch=1,
            grid=grid,
            in_specs=in_specs,
            out_specs=out_specs,
            scratch_shapes=list(scratch),
        ),
        compiler_params=pltpu.CompilerParams(
            dimension_semantics=("arbitrary",) * len(grid), vmem_limit_bytes=VMEM_LIMIT[name] << 20
        ),
        cost_estimate=pl.CostEstimate(flops=0, bytes_accessed=0, transcendentals=0),
        input_output_aliases=aliases or {},
        name=name,
    )


def sds(shape, dtype):
    return jax.ShapeDtypeStruct(shape, dtype)


def hbm(shape, dtype):
    return pltpu.HBM(shape, dtype)


def const(shape):
    return pl.BlockSpec(shape, lambda i, z: (0,) * len(shape))


def rows_of(shape):
    return pl.BlockSpec(shape, lambda i, z: (i,) + (0,) * (len(shape) - 1))


def lane_ds(start, size):
    return pl.ds(pl.multiple_of(start, 128), size)


def after(value, *others):
    return lax.optimization_barrier((value, others))[0]


def across(value, mask, size):
    return lax.ppermute(value, "tensor", [(i, i ^ mask) for i in range(size)])


def swap(value, mask, size):
    return lax.ppermute(value, "dp", [(i, i ^ mask) for i in range(size)])


def gather4(value, size):
    far = across(value, 2, size)
    near = across(value, 1, size)
    return [value, near, far, across(far, 1, size)]


def scatter4(slots, size):
    got3 = across(slots[3], 1, size)
    got1 = across(slots[1], 1, size)
    far = (slots[2].astype(f32) + got3.astype(f32)).astype(slots[2].dtype)
    return slots[0], got1, across(far, 2, size)


def sum4(value, size):
    value = value + across(value, 1, size)
    return value + across(value, 2, size)


def stages(size):
    bits = list(range(size.bit_length() - 1))
    return [bits[:1]] + [bits[j:j + 2] for j in range(1, len(bits), 2)]


def digit_of(index, group):
    digit = 0
    for j, bit in enumerate(group):
        digit = digit | (((index >> bit) & 1) << j)
    return digit


def mask_of(k, group):
    return sum(((k >> j) & 1) << bit for j, bit in enumerate(group))


def dp_position(size):
    index = lax.axis_index("dp")
    place = 0
    for group in stages(size):
        place = (place << len(group)) | digit_of(index, group)
    return place.astype(jnp.int32)


def dp_scatter(value, size, axis=0, groups=None):
    index = lax.axis_index("dp")
    for group in stages(size) if groups is None else groups:
        n = 1 << len(group)
        mine = digit_of(index, group)
        rows = value.shape[axis] // n
        take = lambda at: lax.dynamic_slice_in_dim(value, at * rows, rows, axis)
        got = [swap(take(mine ^ k), mask_of(k, group), size) for k in range(1, n)]
        total = take(mine).astype(f32)
        for g in got:
            total = total + g.astype(f32)
        value = total.astype(value.dtype)
    return value


def dp_gather_near(value, size):
    value = value[None]
    for group in stages(size)[1:][::-1]:
        n = 1 << len(group)
        value = jnp.stack([value] + [swap(value, mask_of(k, group), size) for k in range(1, n)])
        value = value.reshape((-1,) + value.shape[2:])
    return value


def dp_gather(value, size):
    one = dp_gather_near(value, size)
    return one, swap(one, 1, size)


def dp_sum_small(value, size):
    for bit in range(size.bit_length() - 1):
        value = value + swap(value, 1 << bit, size)
    return value


def k_assemble(axis, p_ref, one, two, *outs):
    n, rows = one.shape[0], one.shape[1 + axis]
    w = outs[0].shape[-1]
    for flip, value in ((0, one), (1, two)):
        for k in range(n):
            at = pl.ds(pl.multiple_of(jnp.bitwise_xor(p_ref[0], flip * n + k) * rows, rows), rows)
            block = value[k]
            for j, out in enumerate(outs):
                out[(slice(None),) * axis + (at,)] = block[..., j * w:(j + 1) * w].astype(out.dtype)


def assemble(pieces, size, dtype, outs=1, axis=0):
    one, two = pieces
    n = 2 * one.shape[0]
    block = list(one.shape[1:])
    if block[axis] % 16:
        order = jnp.bitwise_xor(jnp.arange(n, dtype=jnp.int32), dp_position(size))
        ordered = jnp.moveaxis(jnp.concatenate([one, two], 0)[order], 0, axis)
        shape = block[:axis] + [n * block[axis]] + block[axis + 1:]
        return jnp.split(ordered.reshape(shape).astype(dtype), outs, axis=-1)
    whole = list(block)
    whole[-1] //= outs
    whole[axis] *= n
    return call(
        partial(k_assemble, axis), "assemble", (1,), [const(one.shape)] * 2,
        [const(tuple(whole))] * outs, [sds(tuple(whole), dtype)] * outs, nbytes=12 * one.size,
    )(dp_position(size).reshape(1), one, two)


def norm_stats(x):
    m = jnp.mean(x, axis=-1, keepdims=True)
    c = x - m
    r = lax.rsqrt(jnp.mean(c * c, axis=-1, keepdims=True) + EPS)
    return m, c, r


def k_qkv(z_ref, x0, x1, x2, x3, s0, s1, s2, s3, wqkv,
          x_out, n_out, q_out, k_out, v_out, nl_out, r_out, g_out):
    z = z_ref[0]
    w = x0.shape[1]
    for r, (xb, s) in enumerate(((x0, s0), (x1, s1), (x2, s2), (x3, s3))):
        at = lane_ds(jnp.bitwise_xor(z, r) * w, w)
        x_out[:, at] = xb[...]
        g_out[:, at] = s[0:16, :].astype(f32)
    m, c, r = norm_stats(x_out[...].astype(f32))
    n = (c * r * g_out[0:1, :] + g_out[1:2, :]).astype(bf16)
    n_out[...] = n
    nl_out[...] = (x0[...].astype(f32) - m) * r
    r_out[...] = jnp.broadcast_to(r, r_out.shape)
    small = s0[0:16, :].astype(f32)
    full = mm(n, wqkv[...])
    q_out[...] = ((full[:, :w] + small[5:6, :]).astype(bf16) * 0.125).astype(bf16)
    k_out[...] = full[:, w:2 * w].astype(bf16)
    v_out[...] = (full[:, 2 * w:] + small[6:7, :]).astype(bf16)


def low_lanes(shape):
    return lax.broadcasted_iota(jnp.int32, shape, len(shape) - 1) < HD


def k_attend(z_ref, q, k, v, bias, ctx_out, p_out):
    rows = q.shape[0]
    nblk = rows // BLOCK
    low = low_lanes((rows, 2 * HD))
    heads = q.shape[1] // HD
    for pair in range(heads // 2):
        lanes = slice(pair * 2 * HD, (pair + 1) * 2 * HD)
        qp = q[:, lanes]
        kp = k[:, lanes]
        vp = v[:, lanes]
        parts = []
        for side in range(2):
            h = pair * 2 + side
            qm = jnp.where(low if side == 0 else ~low, qp, jnp.zeros_like(qp))
            s = mm(qm, kp, NT)
            pieces = []
            for b in range(nblk):
                sb = s[b * BLOCK:(b + 1) * BLOCK] + bias[b * heads + h:b * heads + h + 1, :]
                top = jnp.max(sb, axis=-1, keepdims=True)
                e = jnp.exp(sb - top)
                total = jnp.sum(e, axis=-1, keepdims=True)
                pieces.append((e * (1.0 / total)).astype(bf16))
            p = jnp.concatenate(pieces, 0)
            p_out[h] = p
            parts.append(mm(p, vp))
        ctx_out[:, lanes] = jnp.where(low, parts[0], parts[1]).astype(bf16)


def k_ffn(base, z_ref, c0, c1, c2, c3, gs, g_own, x, gains, wo0, wo, wu, ub, wd, *rest):
    (go_out, res_out, n_out, act_out, gup_out, d0, d1, d2, d3,
     h0, h1, h2, h3, sums_out) = rest[-14:]
    i = pl.program_id(0)
    z = z_ref[0]
    w = c0.shape[1]
    attn = mm(c0[...], wo0[...])
    for r, c in enumerate((c1, c2, c3)):
        attn = attn + mm(c[...], wo[r])
    for j in range(gs.shape[0]):
        go_out[:, j * w:(j + 1) * w] = gs[j]
    resid = x[...].astype(f32) + attn + gains[2:3, :]
    res_out[...] = resid
    m, c, r = norm_stats(resid)
    n = (c * r * gains[3:4, :] + gains[4:5, :]).astype(bf16)
    n_out[...] = n
    u = mm(n, wu[...]) + ub[...].astype(f32)
    uu = u * u
    t = jnp.tanh(0.7978845608028654 * u * (1.0 + 0.044715 * uu))
    half = 0.5 * (1.0 + t)
    act = (u * half).astype(bf16)
    slope = half + 0.5 * u * (1.0 - t * t) * (0.7978845608028654 * (1.0 + 0.134145 * uu))
    act_out[...] = act
    gup = (mm(go_out[...], wd[...], NT) * slope).astype(bf16)
    gup_out[...] = gup
    gnt = mm(gup, wu[...], NT).astype(bf16)
    seg = h0.shape[0]
    per = gnt.shape[0] // seg
    for s in range(per):
        for r, h in enumerate((h0, h1, h2, h3)):
            @pl.when(jnp.bitwise_xor(i * per + s, z) == r)
            def _():
                h[...] = gnt[s * seg:(s + 1) * seg]

    own = lane_ds(z * w, w)
    d0[...] = res_out[:, own] + mm(act, wd[:, own]) + gains[7:8, own]
    for r, d in ((1, d1), (2, d2), (3, d3)):
        d[...] = mm(act, wd[:, lane_ds(jnp.bitwise_xor(z, r) * w, w)]).astype(bf16)

    @pl.when(i == 0)
    def _():
        sums_out[...] = jnp.zeros_like(sums_out)

    sums_out[0:1, :] += jnp.sum(gup.astype(f32), axis=0, keepdims=True)
    sums_out[1:2, 0:w] += jnp.sum(g_own[...].astype(f32), axis=0, keepdims=True)


def k_norm_two(z_ref, h0, h1, h2, resid, go, gains, wo0, wo, gr_out, gb_out, o0, o1, o2, o3, sums_out):
    gnt = h0[...].astype(f32) + h1[...].astype(f32) + h2[...].astype(f32)
    m, c, r = norm_stats(resid[...])
    n = c * r
    e = gnt * gains[3:4, :]
    me = jnp.mean(e, axis=-1, keepdims=True)
    mn = jnp.mean(e * n, axis=-1, keepdims=True)
    gres = go[...].astype(f32) + r * (e - me - n * mn)
    gr_out[...] = gres
    gb = gres.astype(bf16)
    gb_out[...] = gb
    sums_out[...] = jnp.zeros_like(sums_out)
    sums_out[0:1, :] = jnp.sum(gnt * n, axis=0, keepdims=True)
    sums_out[1:2, :] = jnp.sum(gnt, axis=0, keepdims=True)
    sums_out[2:3, :] = jnp.sum(gres, axis=0, keepdims=True)
    o0[...] = mm(gb, wo0[...], NT).astype(bf16)
    for k, o in enumerate((o1, o2, o3)):
        o[...] = mm(gb, wo[k], NT).astype(bf16)


def k_dw_out(z_ref, a0, a1, a2, a3, b0, b1, b2, b3, gb_a, gb_b, out):
    gb = jnp.concatenate([gb_a[...], gb_b[...]], axis=0)
    for r, (a, b) in enumerate(((a0, b0), (a1, b1), (a2, b2), (a3, b3))):
        out[r] = mm(jnp.concatenate([a[...], b[...]], axis=0), gb, TN).astype(bf16)


def k_attend_back(z_ref, q, k, v, p_a, p_b, ctx_a, ctx_b, e0, e1, e2, e3, f0, f1, f2, f3,
                  out, sums_out, gc, gs, cx):
    i = pl.program_id(0)
    z = z_ref[0]
    rows = e0.shape[0]
    total = q.shape[0]
    w = out.shape[1] // 3
    half = total // 2
    for h, es in enumerate(((e0, e1, e2, e3), (f0, f1, f2, f3))):
        for j, e in enumerate(es):
            at = h * half + jnp.bitwise_xor(z, j) * rows
            gc[pl.ds(pl.multiple_of(at, rows), rows), :] = e[...]
    cx[:half] = ctx_a[...]
    cx[half:] = ctx_b[...]
    low = low_lanes((total, 2 * HD))
    qp, kp, vp = q[...], k[...], v[...]
    gcv = gc[...]
    prod = gcv.astype(f32) * cx[...].astype(f32)
    gq, gk, gv = [], [], []
    for side in range(2):
        pick = low if side == 0 else ~low
        delta = jnp.sum(jnp.where(pick, prod, 0.0), axis=-1, keepdims=True)
        gm = jnp.where(pick, gcv, jnp.zeros_like(gcv))
        tile = 256
        for t in range(total // tile):
            at = slice(t * tile, (t + 1) * tile)
            gp = mm(gm[at], vp, NT)
            p = p_a if t * tile < half else p_b
            pt = p[side, t * tile % half:t * tile % half + tile, :].astype(f32)
            gs[at, :] = (pt * (gp - delta[at])).astype(bf16)
        gsv = gs[...]
        gq.append(mm(gsv, kp))
        gk.append(mm(qp, gsv, TN))
        gv.append(mm(gcv[:half], p_a[side], TN) + mm(gcv[half:], p_b[side], TN))
    gqv = (jnp.where(low, gq[0], gq[1]) * 0.125).astype(bf16)
    out[:, lane_ds(i * 2 * HD, 2 * HD)] = gqv
    top = lax.broadcasted_iota(jnp.int32, gk[0].shape, 0) < HD
    out[:, lane_ds(w + i * 2 * HD, 2 * HD)] = jnp.where(top, gk[0], gk[1]).T.astype(bf16)
    gvv = jnp.where(top, gv[0], gv[1]).T.astype(bf16)
    out[:, lane_ds(2 * w + i * 2 * HD, 2 * HD)] = gvv
    sums_out[...] = jnp.zeros_like(sums_out)
    sums_out[0:1, :] = jnp.sum(gqv.astype(f32), axis=0, keepdims=True)
    sums_out[1:2, :] = jnp.sum(gvv.astype(f32), axis=0, keepdims=True)


def k_norm_one(z_ref, g, wqkv, x, gains, gres_a, gres_b, sum_a, sum_b, o0, o1, o2, o3, mix, scr):
    i = pl.program_id(0)
    z = z_ref[0]
    w = o0.shape[1]
    gn = mm(g[...], wqkv[...], NT)
    m, c, r = norm_stats(x[...].astype(f32))
    n = c * r
    e = gn * gains[0:1, :]
    se = jnp.sum(e, axis=-1, keepdims=True)
    de = jnp.sum(e * n, axis=-1, keepdims=True)
    rows = gn.shape[0]
    lane = lax.broadcasted_iota(jnp.int32, (rows, 128), 1)
    cols = jnp.where(lane == 0, se, jnp.where(lane == 1, de, 0.0))
    scr[...] = r * e
    seg = gres_a.shape[0]
    per_half = pl.num_programs(0) // 2
    for h, gres in enumerate((gres_a, gres_b)):
        @pl.when(i == h * per_half + (z * seg) // rows)
        def _():
            scr[pl.ds(pl.multiple_of((z * seg) % rows, seg), seg), :] += gres[...]

    for r, o in enumerate((o0, o1, o2, o3)):
        o[...] = scr[:, lane_ds(jnp.bitwise_xor(z, r) * w, w)].astype(bf16)

    @pl.when(i == 0)
    def _():
        mix[2:4, :] = jnp.zeros((2, D), f32)
        mix[4:8, :] = sum_a[0:4, :] + sum_b[0:4, :]

    mix[0:2, lane_ds(i * rows, rows)] = cols.T[0:2, :]
    mix[2:3, :] += jnp.sum(gn * n, axis=0, keepdims=True)
    mix[3:4, :] += jnp.sum(gn, axis=0, keepdims=True)


def k_widen(z_ref, up, down, vec, up_out, down_out):
    up_out[...] = up[...].astype(f32)
    down_out[...] = down[...].astype(f32)


def k_final(z_ref, t0, t1, t2, stats, nl, r, out):
    total = t0[...].astype(f32) + t1[...].astype(f32) + t2[...].astype(f32)
    cols = jnp.concatenate([stats[...]] * 16, 0).T * (1.0 / D)
    out[...] = (total - r[:, 0:1] * (cols[:, 0:1] + nl[...] * cols[:, 1:2])).astype(bf16)


def mask_bias(random_rows, length):
    heads = random_rows.shape[0]
    rows = jnp.arange(NB, dtype=jnp.int32)[:, None]
    cols = jnp.arange(NB, dtype=jnp.int32)[None, :]
    fixed = (
        (rows == 0) | (rows == NB - 1) | (cols == 0) | (cols == NB - 1)
        | (jnp.abs(rows - cols) <= 1)
    )
    chosen = jnp.any(random_rows[:, :, :, None] == cols[0][None, None, None, :], axis=2)
    allowed = jnp.transpose(fixed[None] | chosen, (1, 0, 2)).reshape(NB * heads, NB)
    valid = jnp.arange(LEN, dtype=jnp.int32) < length
    return jnp.where(jnp.repeat(allowed, BLOCK, axis=1) & valid[None, :], 0.0, -1e30).astype(f32)


def make_shards(dp, tp):
    def shards(inputs, lengths, random_blocks, attn_norm_gain, attn_norm_bias, query_weight,
               query_bias, key_weight, value_weight, value_bias, out_weight, out_bias,
               ffn_norm_gain, ffn_norm_bias, up_weight, up_bias, down_weight, down_bias, grad_out):
        tokens, w = inputs.shape
        ff = up_weight.shape[1]
        heads = w // HD
        half = tokens // 2
        quarter = tokens // tp
        tile = 256
        zi = lax.axis_index("tensor")
        z = zi.astype(jnp.int32).reshape(1)
        d_i = lax.axis_index("dp")

        seg = half // tp
        here_dp = dp_position(dp)
        part_rows = w // dp
        wo_part = lax.dynamic_slice_in_dim(out_weight, here_dp * part_rows, part_rows, 0)
        wo_in = jnp.stack([across(wo_part, r, tp) for r in range(1, tp)])
        far_in = across(inputs, 2, tp)
        near_in = across(inputs, 1, tp)
        small = jnp.concatenate(
            [attn_norm_gain, attn_norm_bias, out_bias, ffn_norm_gain, ffn_norm_bias, query_bias,
             value_bias, down_bias, jnp.zeros((8 * w,), bf16)]).reshape(16, w)
        packs = [small] + [across(small, r, tp) for r in range(1, tp)]
        last_in = across(after(far_in, near_in, packs), 1, tp)
        slots = [inputs, near_in, far_in, last_in]
        wo_pieces = dp_gather(wo_in, dp)
        wqkv = jnp.concatenate([query_weight, key_weight, value_weight], 1)
        bias = mask_bias(random_blocks[0], lengths[0])

        tw, td = rows_of((tile, w)), rows_of((tile, D))
        x_full, n_one, q, k, v, n_loc, r_one, gains = call(
            k_qkv, "qkv", (tokens // tile,),
            [tw] * 4 + [const((16, w))] * 4 + [const((D, 3 * w))],
            [td, td, tw, tw, tw, tw, rows_of((tile, 128)), const((16, D))],
            [hbm((tokens, D), bf16), hbm((tokens, D), bf16), sds((tokens, w), bf16),
             sds((tokens, w), bf16), sds((tokens, w), bf16), hbm((tokens, w), f32),
             hbm((tokens, 128), f32), sds((16, D), f32)],
        )(z, *slots, *packs, after(wqkv, bias))
        gos = lax.all_gather(after(grad_out, last_in), "tensor")

        nblk = tile // BLOCK
        att = []
        for h in range(2):
            steps = half // tile
            base = h * steps
            q_in = q if h == 0 else after(q, att[0][0])
            att.append(call(
                k_attend, "attend", (steps,),
                [pl.BlockSpec((tile, w), lambda i, z, base=base: (i + base, 0)),
                 const((tokens, w)), const((tokens, w)),
                 pl.BlockSpec((nblk * heads, LEN), lambda i, z, base=base: (i + base, 0))],
                [tw, pl.BlockSpec((heads, tile, LEN), lambda i, z: (0, i, 0))],
                [sds((half, w), bf16), hbm((heads, half, LEN), bf16)],
                flops=2 * half * LEN * 128 * heads * 2, nbytes=8 << 20,
            )(z, q_in, k, v, bias))
        ctxs = [gather4(att[h][0], tp) for h in range(2)]

        (wo_rest,) = assemble((after(wo_pieces[0], att[1][0]), wo_pieces[1]), dp, bf16, axis=1)

        ffn = []
        carried = []
        for h in range(2):
            steps = half // tile
            base = h * steps
            here = lambda i, z, base=base: (i + base, 0)
            hw, hd, hf = (pl.BlockSpec((tile, n), here) for n in (w, D, ff))
            n_in = 18
            out = call(
                partial(k_ffn, base), "ffn", (steps,),
                [tw] * 4 + [pl.BlockSpec((tp, tile, w), lambda i, z, base=base: (0, i + base, 0)), hw,
                            hd, const((16, D)), const((w, D)), const((tp - 1, w, D)),
                                       const((D, ff)), const((1, ff)), const((ff, D))]
                + [pl.BlockSpec(memory_space=pl.ANY)] * len(carried),
                [hd, hd, hd, hf, hf, hw, hw, hw, hw] + [const((seg, D))] * 4 + [const((8, ff))],
                [hbm((tokens, D), bf16), hbm((tokens, D), f32), hbm((tokens, D), bf16),
                 hbm((tokens, ff), bf16), hbm((tokens, ff), bf16), sds((tokens, w), f32)]
                + [sds((tokens, w), bf16)] * 3 + [sds((seg, D), bf16)] * 4 + [sds((8, ff), f32)],
                flops=2 * half * D * ff * 5, nbytes=24 << 20,
                aliases={14 + j: j for j in range(len(carried))},
            )(z, *ctxs[h], gos, grad_out, x_full, gains, out_weight, wo_rest, up_weight,
              up_bias.reshape(1, ff), down_weight, *carried)
            carried = out[:9]
            ffn.append(out)
        go_full, res_full, n_two, act, gup, d0, d1, d2, d3 = carried

        groups = stages(dp)
        dw_up = mm(n_two, gup, TN).astype(bf16)
        dw_down = mm(act, go_full, TN).astype(bf16)
        g_up, g_down = lax.psum((dw_up, dw_down), "dp")

        two = []
        for h in range(2):
            h0, h1, h2 = scatter4(ffn[h][9:13], tp)
            h0 = after(h0, dw_up, dw_down) if h == 0 else after(h0, two[0][1])
            at_z = pl.BlockSpec((seg, D), lambda i, z, h=h: (h * tp + z[0], 0))
            two.append(call(
                k_norm_two, "norm_two", (1,),
                [const((seg, D))] * 3 + [at_z, at_z, const((16, D)), const((w, D)),
                                         const((tp - 1, w, D))],
                [const((seg, D)), const((seg, D))] + [const((seg, w))] * 4 + [const((8, D))],
                [sds((seg, D), f32), sds((seg, D), bf16)] + [sds((seg, w), bf16)] * 4
                + [sds((8, D), f32)],
                flops=2 * seg * D * D, nbytes=10 << 20,
            )(z, h0, h1, h2, res_full, go_full, gains, out_weight, wo_rest))
        g_ctx = [[two[h][2]] + [across(two[h][2 + r], r, tp) for r in range(1, tp)]
                 for h in range(2)]
        seg_z = pl.BlockSpec((seg, w), lambda i, z: (z[0], 0))
        dw_out = call(
            k_dw_out, "dw_out", (1,), [seg_z] * 8 + [const((seg, D))] * 2, const((tp, w, D)),
            sds((tp, w, D), bf16), flops=2 * 2 * seg * D * D, nbytes=5 << 20,
        )(z, *ctxs[0], *ctxs[1], after(two[0][1], g_ctx[0]), two[1][1])

        pair = pl.BlockSpec((tokens, 2 * HD), lambda i, z: (0, i))
        pairh = pl.BlockSpec((half, 2 * HD), lambda i, z: (0, i))
        probs = pl.BlockSpec((2, half, LEN), lambda i, z: (i, 0, 0))
        out_part = dp_scatter(dw_out, dp, axis=1, groups=groups[:1])
        gqkv, sums_qkv = call(
            k_attend_back, "attend_back", (heads // 2,),
            [pair, pair, pair, probs, probs, pairh, pairh]
            + [pl.BlockSpec((seg, 2 * HD), lambda i, z: (0, i))] * 8,
            [const((tokens, 3 * w)), pl.BlockSpec((8, 2 * HD), lambda i, z: (0, i))],
            [sds((tokens, 3 * w), bf16), sds((8, w), f32)],
            scratch=[pltpu.VMEM((tokens, 2 * HD), bf16), pltpu.VMEM((tokens, LEN), bf16),
                     pltpu.VMEM((tokens, 2 * HD), bf16)],
        )(z, after(q, out_part), k, v, att[0][1], att[1][1], att[0][0], att[1][0], *g_ctx[0], *g_ctx[1])

        (d1, d2, d3) = after((d1, d2, d3), g_ctx)
        down_got3 = across(d3, 1, tp)
        down_got1 = across(d1, 1, tp)
        down_far = (after(d2, gqkv).astype(f32) + down_got3.astype(f32)).astype(bf16)
        down_got2 = across(down_far, 2, tp)
        outputs = (d0 + down_got1.astype(f32) + down_got2.astype(f32)).astype(bf16)
        out_part = dp_scatter(out_part, dp, axis=1, groups=groups[1:])
        g_in = after(gqkv, down_far, down_got1, out_part)
        *contrib, mix = call(
            k_norm_one, "norm_one", (tokens // tile,),
            [rows_of((tile, 3 * w)), const((D, 3 * w)), td, const((16, D)), const((seg, D)),
             const((seg, D)), const((8, D)), const((8, D))],
            [tw] * 4 + [const((8, D))], [sds((tokens, w), bf16)] * 4 + [sds((8, D), f32)],
            scratch=[pltpu.VMEM((tile, D), f32)],
        )(z, g_in, wqkv, x_full, gains, two[0][0], two[1][0], two[0][6], two[1][6])

        got3 = across(contrib[3], 1, tp)
        got1 = across(contrib[1], 1, tp)
        far = (after(contrib[2], down_got2).astype(f32) + got3.astype(f32)).astype(bf16)
        totals = [contrib[0], got1, across(far, 2, tp)]
        mix = sum4(mix, tp)

        out_got = [across(out_part[r], r, tp) for r in range(1, tp)]
        own = out_part[0].astype(f32)
        for got in out_got:
            own = own + got.astype(f32)
        own = own.astype(bf16)
        dw_qkv = mm(n_one, after(gqkv, contrib), TN).astype(bf16)
        qkv_part = dp_scatter(dw_qkv, dp, groups=groups[:1])
        qkv_part = dp_scatter(after(qkv_part, mix, far, got1, own, g_up), dp, groups=groups[1:])
        out_one, out_two = dp_gather(own, dp)
        (g_out_w,) = assemble((out_one, out_two), dp, f32)
        mine = lax.dynamic_slice(mix, (2, zi * w), (5, w))
        up_sum = ffn[0][-1] + ffn[1][-1]
        vec = jnp.concatenate([mine, sums_qkv[0:2], up_sum[1:2, :w], up_sum[0:1].reshape(-1, w)], 0)
        vec = dp_sum_small(vec, dp)
        qkv_part = after(qkv_part, g_up, totals, vec)
        blocks = rows_of((tile, D))
        g_up, g_down = call(
            k_widen, "widen", (D // tile,), [blocks, blocks, pl.BlockSpec(memory_space=pl.ANY)], [blocks, blocks], [sds((D, ff), f32), sds((ff, D), f32)],
        )(z, g_up, g_down, vec)
        vec = vec.reshape(-1)
        qkv_one = dp_gather_near(after(qkv_part, out_one), dp)
        qkv_two = swap(after(qkv_one, totals, g_out_w, g_up), 1, dp)
        g_q, g_k, g_v = assemble((qkv_one, qkv_two), dp, f32, outs=3)

        grad_inputs = call(
            k_final, "final", (tokens // tile,),
            [tw] * 3 + [pl.BlockSpec((8, tile), lambda i, z: (0, i)), tw, rows_of((tile, 128))],
            tw, sds((tokens, w), bf16),
        )(z, *totals, mix, n_loc, r_one)

        pieces = [vec[j * w:(j + 1) * w] for j in range(8)]
        g_up_b = vec[8 * w:]
        return (outputs, grad_inputs, pieces[0], pieces[1], g_q, pieces[5], g_k, g_v, pieces[6],
                g_out_w, pieces[4], pieces[2], pieces[3], g_up, g_up_b, g_down, pieces[7])

    return shards


def solution(mesh):
    return jax.shard_map(
        make_shards(mesh.shape["dp"], mesh.shape["tensor"]),
        mesh=mesh,
        in_specs=(
            P("dp", "tensor"), P("dp"), P("dp", "tensor", None, None), P("tensor"), P("tensor"),
            P(None, "tensor"), P("tensor"), P(None, "tensor"), P(None, "tensor"), P("tensor"),
            P("tensor", None), P("tensor"), P("tensor"), P("tensor"), P(None, "tensor"),
            P("tensor"), P("tensor", None), P("tensor"), P("dp", "tensor"),
        ),
        out_specs=(
            P("dp", "tensor"), P("dp", "tensor"), P("tensor"), P("tensor"), P(None, "tensor"),
            P("tensor"), P(None, "tensor"), P(None, "tensor"), P("tensor"), P("tensor", None),
            P("tensor"), P("tensor"), P("tensor"), P(None, "tensor"), P("tensor"),
            P("tensor", None), P("tensor"),
        ),
        check_vma=False,
    )
```
